32 devices in a mesh: replica: 8 (over z, y), fsdp: 4 (over x, core).
Axes of the slice: x: 2, y: 2, z: 4, core: 2. Of those that a mesh axis runs over, the one named last changes fastest.
Arguments:
- activations: bfloat16 [8, 512, 8192], P('replica', 'fsdp'), may hold values from -6 to 6
- grad_out: bfloat16 [8, 512, 1024], P('replica', 'fsdp'), may hold values from -6 to 6
- local_weight: bfloat16 [8, 8192, 1024], P('replica', 'fsdp'), may hold values from -6 to 6
- anchor: float32 [8192, 1024], P('fsdp'), may hold values from -6 to 6
- momentum: float32 [8192, 256], P('fsdp'), may hold values from -6 to 6
- projection_key: int32 [2], replicated, may hold values from 0 to 1073741823
Outputs:
- new_anchor: float32 [8192, 1024], P('fsdp')
- new_momentum: float32 [8192, 256], P('fsdp')
The draws below stay inside these ranges and needn't reach their ends.
All inputs are finite; a program needn't handle non-finite values.
Results may differ from the reference program's by a relative error of at most 0.0017.
Values may be sent and summed in bfloat16 or wider, within the bound.
A program may use at most 64 MiB of HBM per device.

```python
import jax
import jax.numpy as jnp
from jax import lax

D = 8192
K = 1024
RANK = 256
TOK_REP = 512
REPLICAS = 8


def steps_of(rng, dims, cuts, smallest, top_value):
    def one(position, shards_of):
        heights = jax.random.uniform(jax.random.fold_in(jax.random.fold_in(rng, 6), position), (shards_of,), jnp.float32, smallest / len(cuts), top_value / len(cuts))
        return jnp.repeat(jnp.exp(heights), dims[position] // shards_of).reshape((-1,) + (1,) * (len(dims) - position - 1))

    loudness = one(*cuts[0])
    for cut in cuts[1:]:
        loudness = loudness * one(*cut)
    return loudness


def centred(own_key, shape, deviation, reach, shards=(), dtype=jnp.bfloat16):
    level = steps_of(own_key, shape, shards, -0.22, 0.18) if shards else 1.0
    values = jax.random.normal(own_key, shape, jnp.float32) * deviation * level
    return jnp.minimum(jnp.maximum(values, -reach), reach).astype(dtype)


def setup_inputs(seed: int = 0) -> dict:
    seeds = jax.random.split(jax.random.key(seed), 7)
    activations = centred(seeds[0], (REPLICAS, TOK_REP, D), 1.0, 6.0, ((0, 8), (1, 4)))
    grad_out = centred(seeds[1], (REPLICAS, TOK_REP, K), 1.0, 6.0, ((0, 8), (1, 4)))
    local_weight = centred(seeds[2], (REPLICAS, D, K), 1.0, 6.0, ((0, 8), (1, 4)))
    anchor = centred(seeds[3], (D, K), 1.0, 6.0, ((0, 4),), jnp.float32)
    momentum = centred(seeds[4], (D, RANK), 1.0, 6.0, ((0, 4),), jnp.float32)
    projection_key = jax.random.randint(seeds[5], (2,), 0, 1073741824).astype(jnp.int32)
    return {"activations": activations, "grad_out": grad_out, "local_weight": local_weight, "anchor": anchor, "momentum": momentum, "projection_key": projection_key}


HIGH = lax.Precision.HIGHEST


def projection(words, rows, cols):
    k_index = lax.broadcasted_iota(jnp.int32, (rows, cols), 0)
    r_index = lax.broadcasted_iota(jnp.int32, (rows, cols), 1)
    hashed = words[0] + k_index * 668265261 + r_index * 374761393 + words[1] * 1103515245
    hashed = jnp.bitwise_xor(hashed, lax.shift_right_logical(hashed, jnp.int32(15)))
    hashed = hashed * 739982445
    hashed = jnp.bitwise_xor(hashed, lax.shift_right_logical(hashed, jnp.int32(12)))
    hashed = hashed * 695938361
    hashed = jnp.bitwise_xor(hashed, lax.shift_right_logical(hashed, jnp.int32(15)))
    level = jnp.bitwise_and(lax.shift_right_logical(hashed, jnp.int32(8)), 65535).astype(jnp.float32)
    return ((level + 0.5) / 65536.0 - 0.5) * (12.0 / rows_rank(cols)) ** 0.5


def rows_rank(cols):
    return float(cols)


def reference(activations, grad_out, local_weight, anchor, momentum, projection_key):
    proj = projection(projection_key, K, RANK)
    scale = float(TOK_REP) ** -0.5
    local_total = jnp.sum(local_weight.astype(jnp.float32), axis=0)
    drift_total = REPLICAS * anchor - local_total

    def one_replica(carry, pair):
        inputs, grads = pair
        projected = jnp.dot(grads.astype(jnp.float32), proj, precision=HIGH)
        part = jnp.dot(inputs.astype(jnp.float32).T, projected, precision=HIGH)
        return carry + part, None

    start = jnp.zeros((D, RANK), jnp.float32)
    grad_total, unused = lax.scan(one_replica, start, (activations, grad_out))
    summed = jnp.dot(drift_total, proj, precision=HIGH) + scale * grad_total
    compressed_mean = summed / REPLICAS
    new_momentum = 0.9 * momentum + compressed_mean
    update = compressed_mean + 0.9 * new_momentum
    new_anchor = anchor - 0.7 * jnp.dot(update, proj.T, precision=HIGH)
    return new_anchor, new_momentum
```

```python
import functools

import jax
import jax.numpy as jnp
from jax import lax
from jax.experimental import pallas as pl
from jax.experimental.pallas import tpu as pltpu
from jax.sharding import PartitionSpec as P

HIGH = lax.Precision.HIGHEST
MESH = pl.DeviceIdType.MESH
CHUNKS = 4
PAD = 16
LEVELS = 32500.0
STEPS = 256.0
NT = (((1,), (1,)), ((), ()))
TN = (((0,), (0,)), ((), ()))


def projection(word0, word1, rows, cols, first=0):
    k_index = lax.broadcasted_iota(jnp.int32, (rows, cols), 0) + first
    r_index = lax.broadcasted_iota(jnp.int32, (rows, cols), 1)
    hashed = word0 + k_index * 668265261 + r_index * 374761393 + word1 * 1103515245
    hashed = jnp.bitwise_xor(hashed, lax.shift_right_logical(hashed, jnp.int32(15)))
    hashed = hashed * 739982445
    hashed = jnp.bitwise_xor(hashed, lax.shift_right_logical(hashed, jnp.int32(12)))
    hashed = hashed * 695938361
    hashed = jnp.bitwise_xor(hashed, lax.shift_right_logical(hashed, jnp.int32(15)))
    level = jnp.bitwise_and(lax.shift_right_logical(hashed, jnp.int32(8)), 65535).astype(
        jnp.float32
    )
    return ((level + 0.5) / 65536.0 - 0.5) * (12.0 / float(cols)) ** 0.5


def split(value):
    high = value.astype(jnp.bfloat16)
    return high, (value - high.astype(jnp.float32)).astype(jnp.bfloat16)


def dot(a, b, dims=(((1,), (0,)), ((), ()))):
    return lax.dot_general(a, b, dims, preferred_element_type=jnp.float32)


def encode(value, ref):
    rows = value.shape[0]
    top = jnp.max(jnp.abs(value), axis=0, keepdims=True)
    power = jnp.ceil(jnp.log(jnp.maximum(top, 1e-30)) * (STEPS * 1.4426950408889634))
    factor = jnp.exp2(power * (-1.0 / STEPS)) * LEVELS
    ref[:rows, :] = jnp.round(value * factor).astype(jnp.int32).astype(jnp.int16)
    ref[rows:, :] = jnp.broadcast_to(
        power.astype(jnp.int32), (PAD, value.shape[1])
    ).astype(jnp.int16)


def decode(ref):
    rows = ref.shape[0] - PAD
    power = ref[rows:, :].astype(jnp.int32).astype(jnp.float32)[:1]
    scale = jnp.exp2(power * (1.0 / STEPS)) * (1.0 / LEVELS)
    return ref[:rows, :].astype(jnp.int32).astype(jnp.float32) * scale


def mean_kernel(
    n_rep, n_y, n_f, key, act, grads, local, anchor, gathered, proj,
    columns, weights, own_anchor, total, pg, grads_in, y_out, y_in, z_out, z_in,
    act_s, act_r, pg_s, pg_r, y1_s, y1_r, z1_s, z1_r, z2_s, z2_r, y2_s, y2_r, here,
):
    n_z = n_rep // n_y
    chunks, tokens_all, width = columns.shape
    tokens = tokens_all // n_f
    half = width // n_y
    block = half // n_z
    depth = weights.shape[2]
    rank = pg.shape[1]
    rep = lax.axis_index("replica")
    f = lax.axis_index("fsdp")
    z, y = rep // n_y, rep % n_y
    other = n_y - 1 - y
    y_peer = {"replica": z * n_y + other}

    def z_peer(d):
        return {"replica": ((z + d) % n_z) * n_y + y}

    barrier = pltpu.get_barrier_semaphore()
    for d in range(1, n_f):
        pl.semaphore_signal(barrier, inc=1, device_id={"fsdp": (f + d) % n_f}, device_id_type=MESH)
    for d in range(1, n_z):
        pl.semaphore_signal(barrier, inc=1, device_id=z_peer(d), device_id_type=MESH)
    pl.semaphore_signal(barrier, inc=1, device_id=y_peer, device_id_type=MESH)

    def remote(src, dst, send, recv, device):
        return pltpu.make_async_remote_copy(
            src_ref=src, dst_ref=dst, send_sem=send, recv_sem=recv,
            device_id=device, device_id_type=MESH,
        )

    mine = pl.ds(pl.multiple_of(f * tokens, tokens), tokens)

    def act_copy(c, d):
        g = (f + d) % n_f
        at = pl.ds(pl.multiple_of((g * chunks + c) * width, width), width)
        return remote(
            act.at[0, :, at], columns.at[c, mine, :], act_s.at[c, d - 1], act_r.at[c, d - 1],
            {"fsdp": g},
        )

    def act_own(c):
        at = pl.ds(pl.multiple_of((f * chunks + c) * width, width), width)
        return pltpu.make_async_copy(act.at[0, :, at], columns.at[c, mine, :], here.at[0, c])

    def weight_copy(c):
        at = pl.ds(pl.multiple_of(c * width, width), width)
        return pltpu.make_async_copy(local.at[0, at, :], weights.at[c], here.at[1, c])

    def anchor_copy(c):
        at = pl.ds(pl.multiple_of(c * width + y * half + z * block, block), block)
        return pltpu.make_async_copy(anchor.at[at, :], own_anchor.at[c], here.at[2, c])

    def pg_copy(d):
        return remote(
            pg.at[mine, :], pg.at[mine, :], pg_s.at[d - 1], pg_r.at[d - 1], {"fsdp": (f + d) % n_f}
        )

    def y1_copy(c):
        return remote(y_out.at[c], y_in.at[c], y1_s.at[c], y1_r.at[c], y_peer)

    def z1_copy(c, d):
        return remote(
            z_out.at[c, d - 1], z_in.at[c, d - 1], z1_s.at[c, d - 1], z1_r.at[c, d - 1], z_peer(d)
        )

    def z2_copy(c, d):
        return remote(
            gathered.at[c, y, z], gathered.at[c, y, z], z2_s.at[c, d - 1], z2_r.at[c, d - 1],
            z_peer(d),
        )

    def y2_copy(c):
        return remote(gathered.at[c, y], gathered.at[c, y], y2_s.at[c], y2_r.at[c], y_peer)

    fetch = pltpu.make_async_copy(grads.at[0], grads_in, here.at[3, 0])
    fetch.start()
    for c in range(chunks):
        weight_copy(c).start()
        act_own(c).start()
        anchor_copy(c).start()
    pl.semaphore_wait(barrier, n_f + n_z - 1)
    order = sorted(range(1, n_f), key=lambda d: abs(d - n_f // 2))
    for d in order:
        act_copy(0, d).start()

    @pl.loop(0, depth, step=rank)
    def _(k):
        at = pl.ds(pl.multiple_of(k, rank), rank)
        high, low = split(projection(key[0], key[1], rank, rank, k))
        proj[at, :rank] = high
        proj[at, rank:] = low

    fetch.wait()
    both = dot(grads_in[...], proj[...])
    pg[mine, :] = (both[:, :rank] + both[:, rank:]).astype(jnp.bfloat16)
    for d in order:
        pg_copy(d).start()
    for c in range(1, chunks):
        for d in order:
            act_copy(c, d).start()

    @pl.loop(0, chunks)
    def _(c):
        weight_copy(c).wait()
        for h in range(n_y):
            at = pl.ds(h * half, half)
            both = dot(weights[c, at, :], proj[...])
            total[c, at, :] = (both[:, :rank] + both[:, rank:]) * (-1.0 / n_rep)

    for d in range(1, n_f):
        pg_copy(d).wait_recv()
    scale = float(tokens_all) ** (-0.5) / n_rep

    @pl.loop(0, chunks + 3)
    def _(t):
        @pl.when(t < chunks)
        def _():
            c = t
            act_own(c).wait()
            for d in range(1, n_f):
                act_copy(c, d).wait_recv()
            total[c] += dot(columns[c], pg[...], TN) * scale
            far = pl.ds(pl.multiple_of(other * half, half), half)
            encode(total[c, far, :], y_out.at[c])
            y1_copy(c).start()

        @pl.when(jnp.logical_and(t >= 1, t < chunks + 1))
        def _():
            c = t - 1
            y1_copy(c).wait_recv()
            near = pl.ds(pl.multiple_of(y * half, half), half)
            total[c, near, :] += decode(y_in.at[c])
            for d in range(1, n_z):
                q = (z + d) % n_z
                at = pl.ds(pl.multiple_of(y * half + q * block, block), block)
                encode(total[c, at, :], z_out.at[c, d - 1])
                z1_copy(c, d).start()

        @pl.when(jnp.logical_and(t >= 2, t < chunks + 2))
        def _():
            c = t - 2
            at = pl.ds(pl.multiple_of(y * half + z * block, block), block)
            anchor_copy(c).wait()
            high, low = split(own_anchor[c])
            both = dot(high, proj[...])
            value = total[c, at, :] + both[:, :rank] + both[:, rank:] + dot(low, proj[:, :rank])
            for d in range(1, n_z):
                z1_copy(c, d).wait_recv()
                value += decode(z_in.at[c, d - 1])
            encode(value, gathered.at[c, y, z])
            for d in range(1, n_z):
                z2_copy(c, d).start()

        @pl.when(t >= 3)
        def _():
            c = t - 3
            for d in range(1, n_z):
                z2_copy(c, d).wait_recv()
            y2_copy(c).start()

    for d in range(1, n_f):
        pg_copy(d).wait_send()

    @pl.loop(0, chunks)
    def _(c):
        for d in range(1, n_f):
            act_copy(c, d).wait_send()
        y1_copy(c).wait_send()
        for d in range(1, n_z):
            z1_copy(c, d).wait_send()
            z2_copy(c, d).wait_send()
        y2_copy(c).wait_send()
        y2_copy(c).wait_recv()


def update_kernel(gathered, proj, anchor, momentum, new_anchor, new_momentum):
    n_z, block = gathered.shape[2], gathered.shape[3] - PAD
    rank = momentum.shape[1]
    for q in range(n_z):
        at = pl.ds(q * block, block)
        mean = decode(gathered.at[0, 0, q])
        moved = 0.9 * momentum[at, :] + mean
        new_momentum[at, :] = moved
    mean = new_momentum[...] - 0.9 * momentum[...]
    high, low = split(mean + 0.9 * new_momentum[...])
    step = dot(high, proj[:, :rank], NT) + dot(high, proj[:, rank:], NT)
    step += dot(low, proj[:, :rank], NT)
    new_anchor[...] = anchor[...] - 0.7 * step


def in_kernels(n_rep, n_y, n_f, act, grads, local, anchor, momentum, key):
    n_z = n_rep // n_y
    rows, depth = anchor.shape
    rank = momentum.shape[1]
    tokens = act.shape[1]
    width = rows // CHUNKS
    half = width // n_y
    block = half // n_z
    dma = pltpu.SemaphoreType.DMA
    any_space = pl.BlockSpec(memory_space=pl.ANY)
    vmem = pl.BlockSpec(memory_space=pltpu.VMEM)
    gathered, proj = pl.pallas_call(
        functools.partial(mean_kernel, n_rep, n_y, n_f),
        out_shape=(
            jax.ShapeDtypeStruct((CHUNKS, n_y, n_z, block + PAD, rank), jnp.int16),
            jax.ShapeDtypeStruct((depth, 2 * rank), jnp.bfloat16),
        ),
        in_specs=[pl.BlockSpec(memory_space=pltpu.SMEM)] + [any_space] * 4,
        out_specs=(vmem, vmem),
        scratch_shapes=[
            pltpu.VMEM((CHUNKS, tokens * n_f, width), jnp.bfloat16),
            pltpu.VMEM((CHUNKS, width, depth), jnp.bfloat16),
            pltpu.VMEM((CHUNKS, block, depth), jnp.float32),
            pltpu.VMEM((CHUNKS, width, rank), jnp.float32),
            pltpu.VMEM((tokens * n_f, rank), jnp.bfloat16),
            pltpu.VMEM((tokens, depth), jnp.bfloat16),
            pltpu.VMEM((CHUNKS, half + PAD, rank), jnp.int16),
            pltpu.VMEM((CHUNKS, half + PAD, rank), jnp.int16),
            pltpu.VMEM((CHUNKS, n_z - 1, block + PAD, rank), jnp.int16),
            pltpu.VMEM((CHUNKS, n_z - 1, block + PAD, rank), jnp.int16),
            dma((CHUNKS, n_f - 1)),
            dma((CHUNKS, n_f - 1)),
            dma((n_f - 1,)),
            dma((n_f - 1,)),
            dma((CHUNKS,)),
            dma((CHUNKS,)),
            dma((CHUNKS, n_z - 1)),
            dma((CHUNKS, n_z - 1)),
            dma((CHUNKS, n_z - 1)),
            dma((CHUNKS, n_z - 1)),
            dma((CHUNKS,)),
            dma((CHUNKS,)),
            dma((4, CHUNKS)),
        ],
        compiler_params=pltpu.CompilerParams(
            collective_id=0, has_side_effects=True, vmem_limit_bytes=40 * 1024 * 1024
        ),
        name="mean",
    )(key, act, grads, local, anchor)

    def tile(i):
        return (i, 0)

    return pl.pallas_call(
        update_kernel,
        grid=(CHUNKS * n_y,),
        out_shape=(
            jax.ShapeDtypeStruct(anchor.shape, anchor.dtype),
            jax.ShapeDtypeStruct(momentum.shape, momentum.dtype),
        ),
        in_specs=[
            pl.BlockSpec((1, 1, n_z, block + PAD, rank), lambda i: (i // n_y, i % n_y, 0, 0, 0)),
            pl.BlockSpec((depth, 2 * rank), lambda i: (0, 0)),
            pl.BlockSpec((half, depth), tile),
            pl.BlockSpec((half, rank), tile),
        ],
        out_specs=(pl.BlockSpec((half, depth), tile), pl.BlockSpec((half, rank), tile)),
        compiler_params=pltpu.CompilerParams(vmem_limit_bytes=32 * 1024 * 1024),
        name="update",
    )(gathered, proj, anchor, momentum)


def in_steps(activations, grad_out, local_weight, anchor, momentum, projection_key):
    inputs = activations[0]
    grads = grad_out[0]
    local = local_weight[0]
    proj = projection(projection_key[0], projection_key[1], grads.shape[1], momentum.shape[1])
    replicas = lax.axis_size("replica")
    scale = float(inputs.shape[0] * lax.axis_size("fsdp")) ** (-0.5)
    drift = anchor - local.astype(jnp.float32)
    columns = lax.all_to_all(inputs, "fsdp", split_axis=1, concat_axis=0, tiled=True)
    projected = jnp.dot(grads.astype(jnp.float32), proj, precision=HIGH)
    grad_part = lax.dot_general(
        columns.astype(jnp.float32),
        lax.all_gather(projected.astype(jnp.bfloat16), "fsdp", axis=0, tiled=True).astype(
            jnp.float32
        ),
        TN,
        precision=HIGH,
        preferred_element_type=jnp.float32,
    )
    local_term = jnp.dot(drift, proj, precision=HIGH) + scale * grad_part
    compressed_mean = lax.psum(local_term, "replica") / replicas
    new_momentum = 0.9 * momentum + compressed_mean
    update = compressed_mean + 0.9 * new_momentum
    new_anchor = anchor - 0.7 * jnp.dot(update, proj.T, precision=HIGH)
    return (new_anchor, new_momentum)


def solution(mesh):
    n_rep, n_f = mesh.shape["replica"], mesh.shape["fsdp"]
    n_y = 2

    def on_device(act, grads, local, anchor, momentum, key):
        rows, depth = anchor.shape
        rank = momentum.shape[1]
        fits = n_rep % n_y == 0 and n_rep > n_y and n_f > 1
        fits = fits and rows % (CHUNKS * n_rep * 16) == 0 and (rows // CHUNKS) % 128 == 0
        fits = fits and act.shape[1] % 16 == 0 and rank % 128 == 0 and depth % rank == 0
        if fits:
            return in_kernels(n_rep, n_y, n_f, act, grads, local, anchor, momentum, key)
        return in_steps(act, grads, local, anchor, momentum, key)

    placed = (
        P("replica", "fsdp", None),
        P("replica", "fsdp", None),
        P("replica", "fsdp", None),
        P("fsdp", None),
        P("fsdp", None),
        P(),
    )
    return jax.shard_map(
        on_device,
        mesh=mesh,
        in_specs=placed,
        out_specs=(P("fsdp", None), P("fsdp", None)),
        check_vma=False,
    )
```

```python
import functools

import jax
import jax.numpy as jnp
from jax import lax
from jax.experimental import pallas as pl
from jax.experimental.pallas import tpu as pltpu
from jax.sharding import PartitionSpec as P

HIGH = lax.Precision.HIGHEST
MESH = pl.DeviceIdType.MESH
CHUNKS = 4
PAD = 16
LANES = 128
LEVELS = 32500.0
STEPS = 256.0
NT = (((1,), (1,)), ((), ()))
TN = (((0,), (0,)), ((), ()))


def projection(word0, word1, rows, cols, first=0):
    k_index = lax.broadcasted_iota(jnp.int32, (rows, cols), 0) + first
    r_index = lax.broadcasted_iota(jnp.int32, (rows, cols), 1)
    hashed = word0 + k_index * 668265261 + r_index * 374761393 + word1 * 1103515245
    hashed = jnp.bitwise_xor(hashed, lax.shift_right_logical(hashed, jnp.int32(15)))
    hashed = hashed * 739982445
    hashed = jnp.bitwise_xor(hashed, lax.shift_right_logical(hashed, jnp.int32(12)))
    hashed = hashed * 695938361
    hashed = jnp.bitwise_xor(hashed, lax.shift_right_logical(hashed, jnp.int32(15)))
    level = jnp.bitwise_and(lax.shift_right_logical(hashed, jnp.int32(8)), 65535).astype(
        jnp.float32
    )
    return ((level + 0.5) / 65536.0 - 0.5) * (12.0 / float(cols)) ** 0.5


def split(value):
    high = value.astype(jnp.bfloat16)
    return high, (value - high.astype(jnp.float32)).astype(jnp.bfloat16)


def dot(a, b, dims=(((1,), (0,)), ((), ()))):
    return lax.dot_general(a, b, dims, preferred_element_type=jnp.float32)


def encode(value, ref):
    rows, cols = value.shape
    top = jnp.max(jnp.abs(value), axis=0, keepdims=True)
    power = jnp.ceil(jnp.log(jnp.maximum(top, 1e-30)) * (STEPS * 1.4426950408889634))
    factor = jnp.exp2(power * (-1.0 / STEPS)) * LEVELS
    coded = jnp.round(value * factor).astype(jnp.int32).astype(jnp.int16)
    line = lax.broadcasted_iota(jnp.int32, (PAD, LANES), 0)
    scales = jnp.zeros((PAD, LANES), jnp.float32)
    for part in range(cols // LANES):
        at = slice(part * LANES, (part + 1) * LANES)
        ref[part * rows : (part + 1) * rows, :] = coded[:, at]
        scales = jnp.where(line == part, power[:, at], scales)
    ref[cols // LANES * rows :, :] = scales.astype(jnp.int32).astype(jnp.int16)


def decode(ref, cols):
    parts = cols // LANES
    rows = (ref.shape[0] - PAD) // parts
    power = ref[parts * rows :, :].astype(jnp.int32).astype(jnp.float32)
    scale = jnp.exp2(power * (1.0 / STEPS)) * (1.0 / LEVELS)
    return jnp.concatenate(
        [
            ref[part * rows : (part + 1) * rows, :].astype(jnp.int32).astype(jnp.float32)
            * scale[part : part + 1]
            for part in range(parts)
        ],
        axis=1,
    )


def mean_kernel(
    n_rep, n_y, n_f, key_hbm, act, grads, local, anchor, gathered, proj,
    key, columns, weights, own_anchor, total, pg, grads_in, y_out, y_in, z_out, z_in,
    act_s, act_r, pg_s, pg_r, y1_s, y1_r, z1_s, z1_r, z2_s, z2_r, y2_s, y2_r, here,
):
    n_z = n_rep // n_y
    chunks, tokens_all, width = columns.shape
    tokens = tokens_all // n_f
    half = width // n_y
    block = half // n_z
    depth = weights.shape[2]
    rank = pg.shape[1]
    rep = lax.axis_index("replica")
    f = lax.axis_index("fsdp")
    z, y = rep // n_y, rep % n_y
    other = n_y - 1 - y
    y_peer = {"replica": z * n_y + other}

    def z_peer(d):
        return {"replica": ((z + d) % n_z) * n_y + y}

    barrier = pltpu.get_barrier_semaphore()
    for d in range(1, n_f):
        pl.semaphore_signal(barrier, inc=1, device_id={"fsdp": (f + d) % n_f}, device_id_type=MESH)
    for d in range(1, n_z):
        pl.semaphore_signal(barrier, inc=1, device_id=z_peer(d), device_id_type=MESH)
    pl.semaphore_signal(barrier, inc=1, device_id=y_peer, device_id_type=MESH)

    def remote(src, dst, send, recv, device):
        return pltpu.make_async_remote_copy(
            src_ref=src, dst_ref=dst, send_sem=send, recv_sem=recv,
            device_id=device, device_id_type=MESH,
        )

    mine = pl.ds(pl.multiple_of(f * tokens, tokens), tokens)

    def act_copy(c, d):
        g = (f + d) % n_f
        at = pl.ds(pl.multiple_of((g * chunks + c) * width, width), width)
        return remote(
            act.at[0, :, at], columns.at[c, mine, :], act_s.at[c, d - 1], act_r.at[c, d - 1],
            {"fsdp": g},
        )

    def act_own(c):
        at = pl.ds(pl.multiple_of((f * chunks + c) * width, width), width)
        return pltpu.make_async_copy(act.at[0, :, at], columns.at[c, mine, :], here.at[0, c])

    def weight_copy(c):
        at = pl.ds(pl.multiple_of(c * width, width), width)
        return pltpu.make_async_copy(local.at[0, at, :], weights.at[c], here.at[1, c])

    def anchor_copy(c):
        at = pl.ds(pl.multiple_of(c * width + y * half + z * block, block), block)
        return pltpu.make_async_copy(anchor.at[at, :], own_anchor.at[c], here.at[2, c])

    def pg_copy(d):
        return remote(
            pg.at[mine, :], pg.at[mine, :], pg_s.at[d - 1], pg_r.at[d - 1], {"fsdp": (f + d) % n_f}
        )

    def y1_copy(c):
        return remote(y_out.at[c], y_in.at[c], y1_s.at[c], y1_r.at[c], y_peer)

    def z1_copy(c, d):
        return remote(
            z_out.at[c, d - 1], z_in.at[c, d - 1], z1_s.at[c, d - 1], z1_r.at[c, d - 1], z_peer(d)
        )

    def z2_copy(c, d):
        return remote(
            gathered.at[c, y, z], gathered.at[c, y, z], z2_s.at[c, d - 1], z2_r.at[c, d - 1],
            z_peer(d),
        )

    def y2_copy(c):
        return remote(gathered.at[c, y], gathered.at[c, y], y2_s.at[c], y2_r.at[c], y_peer)

    fetch = pltpu.make_async_copy(grads.at[0], grads_in, here.at[3, 0])
    fetch.start()
    words = pltpu.make_async_copy(key_hbm, key, here.at[3, 1])
    words.start()
    for c in range(chunks):
        weight_copy(c).start()
        act_own(c).start()
        anchor_copy(c).start()
    pl.semaphore_wait(barrier, n_f + n_z - 1)
    order = sorted(range(1, n_f), key=lambda d: abs(d - n_f // 2))
    for d in order:
        act_copy(0, d).start()
    words.wait()

    @pl.loop(0, depth, step=rank)
    def _(k):
        at = pl.ds(pl.multiple_of(k, rank), rank)
        high, low = split(projection(key[0], key[1], rank, rank, k))
        proj[at, :rank] = high
        proj[at, rank:] = low

    fetch.wait()
    both = dot(grads_in[...], proj[...])
    pg[mine, :] = (both[:, :rank] + both[:, rank:]).astype(jnp.bfloat16)
    for d in order:
        pg_copy(d).start()
    for d in order:
        act_copy(1, d).start()

    @pl.loop(0, chunks)
    def _(c):
        weight_copy(c).wait()
        for h in range(n_y):
            at = pl.ds(h * half, half)
            both = dot(weights[c, at, :], proj[...])
            total[c, at, :] = (both[:, :rank] + both[:, rank:]) * (-1.0 / n_rep)

    for d in range(1, n_f):
        pg_copy(d).wait_recv()
    scale = float(tokens_all) ** (-0.5) / n_rep

    def partial_sum(c):
        act_own(c).wait()
        for d in range(1, n_f):
            act_copy(c, d).wait_recv()

        @pl.when(c + 2 < chunks)
        def _():
            for d in order:
                act_copy(c + 2, d).start()

        total[c] += dot(columns[c], pg[...], TN) * scale
        far = pl.ds(pl.multiple_of(other * half, half), half)
        encode(total[c, far, :], y_out.at[c])
        y1_copy(c).start()

    def sum_of_pair(c):
        y1_copy(c).wait_recv()
        near = pl.ds(pl.multiple_of(y * half, half), half)
        total[c, near, :] += decode(y_in.at[c], rank)
        for d in range(1, n_z):
            q = (z + d) % n_z
            at = pl.ds(pl.multiple_of(y * half + q * block, block), block)
            encode(total[c, at, :], z_out.at[c, d - 1])
            z1_copy(c, d).start()

    def whole_mean(c):
        at = pl.ds(pl.multiple_of(y * half + z * block, block), block)
        anchor_copy(c).wait()
        high, low = split(own_anchor[c])
        both = dot(high, proj[...])
        value = total[c, at, :] + both[:, :rank] + both[:, rank:] + dot(low, proj[:, :rank])
        for d in range(1, n_z):
            z1_copy(c, d).wait_recv()
            value += decode(z_in.at[c, d - 1], rank)
        encode(value, gathered.at[c, y, z])
        for d in range(1, n_z):
            z2_copy(c, d).start()

    def hand_over(c):
        for d in range(1, n_z):
            z2_copy(c, d).wait_recv()
        y2_copy(c).start()

    stages = ((partial_sum, 0), (hand_over, 2), (whole_mean, 1), (sum_of_pair, 0))

    @pl.loop(0, chunks + 2)
    def _(t):
        for stage, lag in stages:

            @pl.when(jnp.logical_and(t >= lag, t < chunks + lag))
            def _(stage=stage, lag=lag):
                stage(t - lag)

    for d in range(1, n_f):
        pg_copy(d).wait_send()

    @pl.loop(0, chunks)
    def _(c):
        for d in range(1, n_f):
            act_copy(c, d).wait_send()
        y1_copy(c).wait_send()
        for d in range(1, n_z):
            z1_copy(c, d).wait_send()
            z2_copy(c, d).wait_send()
        y2_copy(c).wait_send()
        y2_copy(c).wait_recv()


def update_kernel(
    gathered, proj, anchor, momentum, new_anchor, new_momentum, anchor_out, momentum_out, sems
):
    chunks, n_y, n_z = gathered.shape[:3]
    rank = momentum.shape[1]
    width = momentum.shape[0] // chunks
    block = width // n_y // n_z

    def stores(c):
        at = pl.ds(pl.multiple_of(c * width, width), width)
        slot = c % 2
        return (
            pltpu.make_async_copy(anchor_out.at[slot], new_anchor.at[at, :], sems.at[0, slot]),
            pltpu.make_async_copy(momentum_out.at[slot], new_momentum.at[at, :], sems.at[1, slot]),
        )

    @pl.loop(0, chunks)
    def _(c):
        slot = c % 2

        @pl.when(c >= 2)
        def _():
            for store in stores(c - 2):
                store.wait()

        mean = jnp.concatenate(
            [decode(gathered.at[c, h, q], rank) for h in range(n_y) for q in range(n_z)], axis=0
        )
        at = pl.ds(pl.multiple_of(c * width, width), width)
        moved = 0.9 * momentum[at, :] + mean
        momentum_out[slot] = moved
        high, low = split(mean + 0.9 * moved)
        step = dot(jnp.concatenate([high, high], axis=1), proj[...], NT)
        step += dot(low, proj[:, :rank], NT)
        anchor_out[slot] = anchor[at, :] - 0.7 * step
        for store in stores(c):
            store.start()

    for c in range(max(chunks - 2, 0), chunks):
        for store in stores(c):
            store.wait()


def in_kernels(n_rep, n_y, n_f, act, grads, local, anchor, momentum, key):
    n_z = n_rep // n_y
    rows, depth = anchor.shape
    rank = momentum.shape[1]
    tokens = act.shape[1]
    width = rows // CHUNKS
    half = width // n_y
    block = half // n_z
    dma = pltpu.SemaphoreType.DMA
    hbm = pl.BlockSpec(memory_space=pltpu.HBM)
    coded = rank // LANES
    vmem = pl.BlockSpec(memory_space=pltpu.VMEM)
    gathered, proj = pl.pallas_call(
        functools.partial(mean_kernel, n_rep, n_y, n_f),
        out_shape=(
            jax.ShapeDtypeStruct((CHUNKS, n_y, n_z, coded * block + PAD, LANES), jnp.int16),
            jax.ShapeDtypeStruct((depth, 2 * rank), jnp.bfloat16),
        ),
        in_specs=[hbm] * 5,
        out_specs=(vmem, vmem),
        scratch_shapes=[
            pltpu.SMEM(key.shape, jnp.int32),
            pltpu.VMEM((CHUNKS, tokens * n_f, width), jnp.bfloat16),
            pltpu.VMEM((CHUNKS, width, depth), jnp.bfloat16),
            pltpu.VMEM((CHUNKS, block, depth), jnp.float32),
            pltpu.VMEM((CHUNKS, width, rank), jnp.float32),
            pltpu.VMEM((tokens * n_f, rank), jnp.bfloat16),
            pltpu.VMEM((tokens, depth), jnp.bfloat16),
            pltpu.VMEM((CHUNKS, coded * half + PAD, LANES), jnp.int16),
            pltpu.VMEM((CHUNKS, coded * half + PAD, LANES), jnp.int16),
            pltpu.VMEM((CHUNKS, n_z - 1, coded * block + PAD, LANES), jnp.int16),
            pltpu.VMEM((CHUNKS, n_z - 1, coded * block + PAD, LANES), jnp.int16),
            dma((CHUNKS, n_f - 1)),
            dma((CHUNKS, n_f - 1)),
            dma((n_f - 1,)),
            dma((n_f - 1,)),
            dma((CHUNKS,)),
            dma((CHUNKS,)),
            dma((CHUNKS, n_z - 1)),
            dma((CHUNKS, n_z - 1)),
            dma((CHUNKS, n_z - 1)),
            dma((CHUNKS, n_z - 1)),
            dma((CHUNKS,)),
            dma((CHUNKS,)),
            dma((4, CHUNKS)),
        ],
        compiler_params=pltpu.CompilerParams(
            collective_id=0, has_side_effects=True, vmem_limit_bytes=52844 * 1024
        ),
        name="mean",
    )(key, act, grads, local, anchor)

    return pl.pallas_call(
        update_kernel,
        out_shape=(
            jax.ShapeDtypeStruct(anchor.shape, anchor.dtype),
            jax.ShapeDtypeStruct(momentum.shape, momentum.dtype),
        ),
        in_specs=[vmem] * 4,
        out_specs=(hbm, hbm),
        scratch_shapes=[
            pltpu.VMEM((2, width, depth), jnp.float32),
            pltpu.VMEM((2, width, rank), jnp.float32),
            dma((2, 2)),
        ],
        compiler_params=pltpu.CompilerParams(vmem_limit_bytes=32 * 1024 * 1024),
        name="update",
    )(gathered, proj, anchor, momentum)


def in_steps(activations, grad_out, local_weight, anchor, momentum, projection_key):
    inputs = activations[0]
    grads = grad_out[0]
    local = local_weight[0]
    proj = projection(projection_key[0], projection_key[1], grads.shape[1], momentum.shape[1])
    replicas = lax.axis_size("replica")
    scale = float(inputs.shape[0] * lax.axis_size("fsdp")) ** (-0.5)
    drift = anchor - local.astype(jnp.float32)
    columns = lax.all_to_all(inputs, "fsdp", split_axis=1, concat_axis=0, tiled=True)
    projected = jnp.dot(grads.astype(jnp.float32), proj, precision=HIGH)
    grad_part = lax.dot_general(
        columns.astype(jnp.float32),
        lax.all_gather(projected.astype(jnp.bfloat16), "fsdp", axis=0, tiled=True).astype(
            jnp.float32
        ),
        TN,
        precision=HIGH,
        preferred_element_type=jnp.float32,
    )
    local_term = jnp.dot(drift, proj, precision=HIGH) + scale * grad_part
    compressed_mean = lax.psum(local_term, "replica") / replicas
    new_momentum = 0.9 * momentum + compressed_mean
    update = compressed_mean + 0.9 * new_momentum
    new_anchor = anchor - 0.7 * jnp.dot(update, proj.T, precision=HIGH)
    return (new_anchor, new_momentum)


def solution(mesh):
    n_rep, n_f = mesh.shape["replica"], mesh.shape["fsdp"]
    n_y = 2

    def on_device(act, grads, local, anchor, momentum, key):
        rows, depth = anchor.shape
        rank = momentum.shape[1]
        fits = n_rep % n_y == 0 and n_rep > n_y and n_f > 1
        fits = fits and rows % (CHUNKS * n_rep * 16) == 0 and (rows // CHUNKS) % 128 == 0
        fits = fits and act.shape[1] % 16 == 0 and rank % 128 == 0 and depth % rank == 0
        if fits:
            return in_kernels(n_rep, n_y, n_f, act, grads, local, anchor, momentum, key)
        return in_steps(act, grads, local, anchor, momentum, key)

    placed = (
        P("replica", "fsdp", None),
        P("replica", "fsdp", None),
        P("replica", "fsdp", None),
        P("fsdp", None),
        P("fsdp", None),
        P(),
    )
    return jax.shard_map(
        on_device,
        mesh=mesh,
        in_specs=placed,
        out_specs=(P("fsdp", None), P("fsdp", None)),
        check_vma=False,
    )
```

```python
import functools

import jax
import jax.numpy as jnp
from jax import lax
from jax.experimental import pallas as pl
from jax.experimental.pallas import tpu as pltpu
from jax.sharding import PartitionSpec as P

HIGH = lax.Precision.HIGHEST
MESH = pl.DeviceIdType.MESH
CHUNKS = 8
AHEAD = 3
GROUP = 2
PAD = 16
LANES = 128
LEVELS = 32500.0
STEPS = 256.0
TN = (((0,), (0,)), ((), ()))


def projection(word0, word1, rows, cols, first=0, turned=False):
    shape = (cols, rows) if turned else (rows, cols)
    k_index = lax.broadcasted_iota(jnp.int32, shape, int(turned)) + first
    r_index = lax.broadcasted_iota(jnp.int32, shape, int(not turned))
    hashed = word0 + k_index * 668265261 + r_index * 374761393 + word1 * 1103515245
    hashed = jnp.bitwise_xor(hashed, lax.shift_right_logical(hashed, jnp.int32(15)))
    hashed = hashed * 739982445
    hashed = jnp.bitwise_xor(hashed, lax.shift_right_logical(hashed, jnp.int32(12)))
    hashed = hashed * 695938361
    hashed = jnp.bitwise_xor(hashed, lax.shift_right_logical(hashed, jnp.int32(15)))
    level = jnp.bitwise_and(lax.shift_right_logical(hashed, jnp.int32(8)), 65535).astype(
        jnp.float32
    )
    return ((level + 0.5) / 65536.0 - 0.5) * (12.0 / float(cols)) ** 0.5


def split(value):
    high = value.astype(jnp.bfloat16)
    return high, (value - high.astype(jnp.float32)).astype(jnp.bfloat16)


def dot(a, b, dims=(((1,), (0,)), ((), ()))):
    return lax.dot_general(a, b, dims, preferred_element_type=jnp.float32)


def encode(value, ref):
    rows, cols = value.shape
    top = jnp.max(jnp.abs(value), axis=0, keepdims=True)
    power = jnp.ceil(jnp.log(jnp.maximum(top, 1e-30)) * (STEPS * 1.4426950408889634))
    factor = jnp.exp2(power * (-1.0 / STEPS)) * LEVELS
    coded = jnp.round(value * factor).astype(jnp.int32).astype(jnp.int16)
    line = lax.broadcasted_iota(jnp.int32, (PAD, LANES), 0)
    scales = jnp.zeros((PAD, LANES), jnp.float32)
    for part in range(cols // LANES):
        at = slice(part * LANES, (part + 1) * LANES)
        ref[part * rows : (part + 1) * rows, :] = coded[:, at]
        scales = jnp.where(line == part, power[:, at], scales)
    ref[cols // LANES * rows :, :] = scales.astype(jnp.int32).astype(jnp.int16)


def decode(ref, cols):
    parts = cols // LANES
    rows = (ref.shape[0] - PAD) // parts
    power = ref[parts * rows :, :].astype(jnp.int32).astype(jnp.float32)
    scale = jnp.exp2(power * (1.0 / STEPS)) * (1.0 / LEVELS)
    return jnp.concatenate(
        [
            ref[part * rows : (part + 1) * rows, :].astype(jnp.int32).astype(jnp.float32)
            * scale[part : part + 1]
            for part in range(parts)
        ],
        axis=1,
    )


def mean_kernel(
    n_rep, n_y, n_f, key_hbm, act, grads, local, anchor, gathered, turned,
    key, proj, columns, weights, own_anchor, total, pg, grads_in, y_out, y_in, z_out, z_in,
    act_s, act_r, pg_s, pg_r, y1_s, y1_r, z1_s, z1_r, z2_s, z2_r, y2_s, y2_r, here,
):
    n_z = n_rep // n_y
    chunks, tokens_all, width = columns.shape
    tokens = tokens_all // n_f
    half = width // n_y
    block = half // n_z
    depth = weights.shape[2]
    rank = pg.shape[1]
    rep = lax.axis_index("replica")
    f = lax.axis_index("fsdp")
    z, y = rep // n_y, rep % n_y
    other = n_y - 1 - y
    y_peer = {"replica": z * n_y + other}

    def z_peer(d):
        return {"replica": ((z + d) % n_z) * n_y + y}

    barrier = pltpu.get_barrier_semaphore()
    for d in range(1, n_f):
        pl.semaphore_signal(barrier, inc=1, device_id={"fsdp": (f + d) % n_f}, device_id_type=MESH)
    for d in range(1, n_z):
        pl.semaphore_signal(barrier, inc=1, device_id=z_peer(d), device_id_type=MESH)
    pl.semaphore_signal(barrier, inc=1, device_id=y_peer, device_id_type=MESH)

    def remote(src, dst, send, recv, device):
        return pltpu.make_async_remote_copy(
            src_ref=src, dst_ref=dst, send_sem=send, recv_sem=recv,
            device_id=device, device_id_type=MESH,
        )

    mine = pl.ds(pl.multiple_of(f * tokens, tokens), tokens)

    def act_copy(c, d):
        g = (f + d) % n_f
        at = pl.ds(pl.multiple_of((g * chunks + c) * width, width), width)
        return remote(
            act.at[0, :, at], columns.at[c, mine, :], act_s.at[c, d - 1], act_r.at[c, d - 1],
            {"fsdp": g},
        )

    def act_own(c):
        at = pl.ds(pl.multiple_of((f * chunks + c) * width, width), width)
        return pltpu.make_async_copy(act.at[0, :, at], columns.at[c, mine, :], here.at[0, c])

    def weight_copy(c):
        at = pl.ds(pl.multiple_of(c * width, width), width)
        return pltpu.make_async_copy(local.at[0, at, :], weights.at[c], here.at[1, c])

    def anchor_copy(c):
        at = pl.ds(pl.multiple_of(c * width + y * half + z * block, block), block)
        return pltpu.make_async_copy(anchor.at[at, :], own_anchor.at[c], here.at[2, c])

    def pg_copy(d):
        return remote(
            pg.at[mine, :], pg.at[mine, :], pg_s.at[d - 1], pg_r.at[d - 1], {"fsdp": (f + d) % n_f}
        )

    def y1_copy(c):
        return remote(y_out.at[c], y_in.at[c], y1_s.at[c], y1_r.at[c], y_peer)

    def z1_copy(c, d):
        return remote(
            z_out.at[c, d - 1], z_in.at[c, d - 1], z1_s.at[c, d - 1], z1_r.at[c, d - 1], z_peer(d)
        )

    def z2_copy(c, d):
        return remote(
            gathered.at[c, y, z], gathered.at[c, y, z], z2_s.at[c, d - 1], z2_r.at[c, d - 1],
            z_peer(d),
        )

    def y2_copy(c):
        return remote(gathered.at[c, y], gathered.at[c, y], y2_s.at[c], y2_r.at[c], y_peer)

    fetch = pltpu.make_async_copy(grads.at[0], grads_in, here.at[3, 0])
    fetch.start()
    words = pltpu.make_async_copy(key_hbm, key, here.at[3, 1])
    words.start()
    for c in range(chunks):
        weight_copy(c).start()
        act_own(c).start()
        anchor_copy(c).start()
    pl.semaphore_wait(barrier, n_f + n_z - 1)
    order = sorted(range(1, n_f), key=lambda d: abs(d - n_f // 2))
    for d in order:
        act_copy(0, d).start()
    words.wait()

    @pl.loop(0, depth, step=rank)
    def _(k):
        at = pl.ds(pl.multiple_of(k, rank), rank)
        high, low = split(projection(key[0], key[1], rank, rank, k))
        proj[at, :rank] = high
        proj[at, rank:] = low

    fetch.wait()
    both = dot(grads_in[...], proj[...])
    pg[mine, :] = (both[:, :rank] + both[:, rank:]).astype(jnp.bfloat16)
    for d in order:
        pg_copy(d).start()
    for c in range(1, min(AHEAD, chunks)):
        for d in order:
            act_copy(c, d).start()

    @pl.loop(0, chunks)
    def _(c):
        weight_copy(c).wait()
        both = dot(weights[c], proj[...])
        total[c] = (both[:, :rank] + both[:, rank:]) * (-1.0 / n_rep)

    for k in range(0, depth, rank):
        high, low = split(projection(key[0], key[1], rank, rank, k, True))
        turned[:rank, k : k + rank] = high
        turned[rank : 2 * rank, k : k + rank] = low
        turned[2 * rank :, k : k + rank] = high
    for d in range(1, n_f):
        pg_copy(d).wait_recv()
    scale = float(tokens_all) ** (-0.5) / n_rep

    def partial_sum(c):
        act_own(c).wait()
        for d in range(1, n_f):
            act_copy(c, d).wait_recv()

        @pl.when(c + AHEAD < chunks)
        def _():
            for d in order:
                act_copy(c + AHEAD, d).start()

        total[c] += dot(columns[c], pg[...], TN) * scale
        far = pl.ds(pl.multiple_of(other * half, half), half)
        encode(total[c, far, :], y_out.at[c])
        y1_copy(c).start()

    def sum_of_pair(c):
        y1_copy(c).wait_recv()
        near = pl.ds(pl.multiple_of(y * half, half), half)
        total[c, near, :] += decode(y_in.at[c], rank)
        for d in range(1, n_z):
            q = (z + d) % n_z
            at = pl.ds(pl.multiple_of(y * half + q * block, block), block)
            encode(total[c, at, :], z_out.at[c, d - 1])
            z1_copy(c, d).start()

    def whole_mean(c):
        at = pl.ds(pl.multiple_of(y * half + z * block, block), block)
        anchor_copy(c).wait()
        high, low = split(own_anchor[c])
        both = dot(high, proj[...])
        value = total[c, at, :] + both[:, :rank] + both[:, rank:] + dot(low, proj[:, :rank])
        for d in range(1, n_z):
            z1_copy(c, d).wait_recv()
            value += decode(z_in.at[c, d - 1], rank)
        encode(value, gathered.at[c, y, z])
        for d in range(1, n_z):
            z2_copy(c, d).start()

    def hand_over(c):
        for d in range(1, n_z):
            z2_copy(c, d).wait_recv()
        y2_copy(c).start()

    stages = ((partial_sum, 0), (hand_over, 4), (sum_of_pair, 1), (whole_mean, 2))

    @pl.loop(0, chunks + 4)
    def _(t):
        for stage, lag in stages:

            @pl.when(jnp.logical_and(t >= lag, t < chunks + lag))
            def _(stage=stage, lag=lag):
                stage(t - lag)

    for d in range(1, n_f):
        pg_copy(d).wait_send()

    @pl.loop(0, chunks)
    def _(c):
        for d in range(1, n_f):
            act_copy(c, d).wait_send()
        y1_copy(c).wait_send()
        for d in range(1, n_z):
            z1_copy(c, d).wait_send()
            z2_copy(c, d).wait_send()
        y2_copy(c).wait_send()
        y2_copy(c).wait_recv()


def update_kernel(
    gathered, turned, anchor, momentum, new_anchor, new_momentum, anchor_out, momentum_out, sems
):
    chunks, n_y, n_z = gathered.shape[:3]
    rank = momentum.shape[1]
    steps = chunks // GROUP
    width = momentum.shape[0] // steps

    def stores(c):
        at = pl.ds(pl.multiple_of(c * width, width), width)
        slot = c % 2
        return (
            pltpu.make_async_copy(anchor_out.at[slot], new_anchor.at[at, :], sems.at[0, slot]),
            pltpu.make_async_copy(momentum_out.at[slot], new_momentum.at[at, :], sems.at[1, slot]),
        )

    @pl.loop(0, steps)
    def _(c):
        slot = c % 2

        @pl.when(c >= 2)
        def _():
            for store in stores(c - 2):
                store.wait()

        mean = jnp.concatenate(
            [
                decode(gathered.at[c * GROUP + g, h, q], rank)
                for g in range(GROUP)
                for h in range(n_y)
                for q in range(n_z)
            ],
            axis=0,
        )
        at = pl.ds(pl.multiple_of(c * width, width), width)
        moved = 0.9 * momentum[at, :] + mean
        momentum_out[slot] = moved
        high, low = split(mean + 0.9 * moved)
        step = dot(jnp.concatenate([high, high, low], axis=1), turned[...])
        anchor_out[slot] = anchor[at, :] - 0.7 * step
        for store in stores(c):
            store.start()

    for c in range(max(steps - 2, 0), steps):
        for store in stores(c):
            store.wait()


def in_kernels(n_rep, n_y, n_f, act, grads, local, anchor, momentum, key):
    n_z = n_rep // n_y
    rows, depth = anchor.shape
    rank = momentum.shape[1]
    tokens = act.shape[1]
    width = rows // CHUNKS
    half = width // n_y
    block = half // n_z
    dma = pltpu.SemaphoreType.DMA
    hbm = pl.BlockSpec(memory_space=pltpu.HBM)
    coded = rank // LANES
    vmem = pl.BlockSpec(memory_space=pltpu.VMEM)
    gathered, turned = pl.pallas_call(
        functools.partial(mean_kernel, n_rep, n_y, n_f),
        out_shape=(
            jax.ShapeDtypeStruct((CHUNKS, n_y, n_z, coded * block + PAD, LANES), jnp.int16),
            jax.ShapeDtypeStruct((3 * rank, depth), jnp.bfloat16),
        ),
        in_specs=[hbm] * 5,
        out_specs=(vmem, vmem),
        scratch_shapes=[
            pltpu.SMEM(key.shape, jnp.int32),
            pltpu.VMEM((depth, 2 * rank), jnp.bfloat16),
            pltpu.VMEM((CHUNKS, tokens * n_f, width), jnp.bfloat16),
            pltpu.VMEM((CHUNKS, width, depth), jnp.bfloat16),
            pltpu.VMEM((CHUNKS, block, depth), jnp.float32),
            pltpu.VMEM((CHUNKS, width, rank), jnp.float32),
            pltpu.VMEM((tokens * n_f, rank), jnp.bfloat16),
            pltpu.VMEM((tokens, depth), jnp.bfloat16),
            pltpu.VMEM((CHUNKS, coded * half + PAD, LANES), jnp.int16),
            pltpu.VMEM((CHUNKS, coded * half + PAD, LANES), jnp.int16),
            pltpu.VMEM((CHUNKS, n_z - 1, coded * block + PAD, LANES), jnp.int16),
            pltpu.VMEM((CHUNKS, n_z - 1, coded * block + PAD, LANES), jnp.int16),
            dma((CHUNKS, n_f - 1)),
            dma((CHUNKS, n_f - 1)),
            dma((n_f - 1,)),
            dma((n_f - 1,)),
            dma((CHUNKS,)),
            dma((CHUNKS,)),
            dma((CHUNKS, n_z - 1)),
            dma((CHUNKS, n_z - 1)),
            dma((CHUNKS, n_z - 1)),
            dma((CHUNKS, n_z - 1)),
            dma((CHUNKS,)),
            dma((CHUNKS,)),
            dma((4, CHUNKS)),
        ],
        compiler_params=pltpu.CompilerParams(
            collective_id=0, has_side_effects=True, vmem_limit_bytes=51700 * 1024
        ),
        name="mean",
    )(key, act, grads, local, anchor)

    return pl.pallas_call(
        update_kernel,
        out_shape=(
            jax.ShapeDtypeStruct(anchor.shape, anchor.dtype),
            jax.ShapeDtypeStruct(momentum.shape, momentum.dtype),
        ),
        in_specs=[vmem] * 4,
        out_specs=(hbm, hbm),
        scratch_shapes=[
            pltpu.VMEM((2, GROUP * width, depth), jnp.float32),
            pltpu.VMEM((2, GROUP * width, rank), jnp.float32),
            dma((2, 2)),
        ],
        compiler_params=pltpu.CompilerParams(vmem_limit_bytes=32 * 1024 * 1024),
        name="update",
    )(gathered, turned, anchor, momentum)


def in_steps(activations, grad_out, local_weight, anchor, momentum, projection_key):
    inputs = activations[0]
    grads = grad_out[0]
    local = local_weight[0]
    proj = projection(projection_key[0], projection_key[1], grads.shape[1], momentum.shape[1])
    replicas = lax.axis_size("replica")
    scale = float(inputs.shape[0] * lax.axis_size("fsdp")) ** (-0.5)
    drift = anchor - local.astype(jnp.float32)
    columns = lax.all_to_all(inputs, "fsdp", split_axis=1, concat_axis=0, tiled=True)
    projected = jnp.dot(grads.astype(jnp.float32), proj, precision=HIGH)
    grad_part = lax.dot_general(
        columns.astype(jnp.float32),
        lax.all_gather(projected.astype(jnp.bfloat16), "fsdp", axis=0, tiled=True).astype(
            jnp.float32
        ),
        TN,
        precision=HIGH,
        preferred_element_type=jnp.float32,
    )
    local_term = jnp.dot(drift, proj, precision=HIGH) + scale * grad_part
    compressed_mean = lax.psum(local_term, "replica") / replicas
    new_momentum = 0.9 * momentum + compressed_mean
    update = compressed_mean + 0.9 * new_momentum
    new_anchor = anchor - 0.7 * jnp.dot(update, proj.T, precision=HIGH)
    return (new_anchor, new_momentum)


def solution(mesh):
    n_rep, n_f = mesh.shape["replica"], mesh.shape["fsdp"]
    n_y = 2

    def on_device(act, grads, local, anchor, momentum, key):
        rows, depth = anchor.shape
        rank = momentum.shape[1]
        fits = n_rep % n_y == 0 and n_rep > n_y and n_f > 1
        fits = fits and rows % (CHUNKS * n_rep * 16) == 0 and (rows // CHUNKS) % 128 == 0
        fits = fits and act.shape[1] % 16 == 0 and rank % 128 == 0 and depth % rank == 0
        if fits:
            return in_kernels(n_rep, n_y, n_f, act, grads, local, anchor, momentum, key)
        return in_steps(act, grads, local, anchor, momentum, key)

    placed = (
        P("replica", "fsdp", None),
        P("replica", "fsdp", None),
        P("replica", "fsdp", None),
        P("fsdp", None),
        P("fsdp", None),
        P(),
    )
    return jax.shard_map(
        on_device,
        mesh=mesh,
        in_specs=placed,
        out_specs=(P("fsdp", None), P("fsdp", None)),
        check_vma=False,
    )
```

```python
import functools

import jax
import jax.numpy as jnp
from jax import lax
from jax.experimental import pallas as pl
from jax.experimental.pallas import tpu as pltpu
from jax.sharding import PartitionSpec as P

HIGH = lax.Precision.HIGHEST
MESH = pl.DeviceIdType.MESH
CHUNKS = 8
AHEAD = 3
GROUP = 2
PAD = 16
LANES = 128
LEVELS = 32500.0
STEPS = 256.0
TN = (((0,), (0,)), ((), ()))


def projection(word0, word1, rows, cols, first=0, turned=False):
    shape = (cols, rows) if turned else (rows, cols)
    k_index = lax.broadcasted_iota(jnp.int32, shape, int(turned)) + first
    r_index = lax.broadcasted_iota(jnp.int32, shape, int(not turned))
    hashed = word0 + k_index * 668265261 + r_index * 374761393 + word1 * 1103515245
    hashed = jnp.bitwise_xor(hashed, lax.shift_right_logical(hashed, jnp.int32(15)))
    hashed = hashed * 739982445
    hashed = jnp.bitwise_xor(hashed, lax.shift_right_logical(hashed, jnp.int32(12)))
    hashed = hashed * 695938361
    hashed = jnp.bitwise_xor(hashed, lax.shift_right_logical(hashed, jnp.int32(15)))
    level = jnp.bitwise_and(lax.shift_right_logical(hashed, jnp.int32(8)), 65535).astype(
        jnp.float32
    )
    return ((level + 0.5) / 65536.0 - 0.5) * (12.0 / float(cols)) ** 0.5


def split(value):
    high = value.astype(jnp.bfloat16)
    return high, (value - high.astype(jnp.float32)).astype(jnp.bfloat16)


def dot(a, b, dims=(((1,), (0,)), ((), ()))):
    return lax.dot_general(a, b, dims, preferred_element_type=jnp.float32)


def encode(value, refs):
    cols = value.shape[1]
    parts, rows = cols // LANES, value.shape[0] // len(refs)
    top = jnp.max(jnp.abs(value), axis=0, keepdims=True)
    power = jnp.ceil(jnp.log(jnp.maximum(top, 1e-30)) * (STEPS * 1.4426950408889634))
    factor = jnp.exp2(power * (-1.0 / STEPS)) * LEVELS
    coded = jnp.round(value * factor).astype(jnp.int32).astype(jnp.int16)
    line = lax.broadcasted_iota(jnp.int32, (PAD, LANES), 0)
    scales = jnp.zeros((PAD, LANES), jnp.float32)
    for part in range(parts):
        scales = jnp.where(line == part, power[:, part * LANES : (part + 1) * LANES], scales)
    scales = scales.astype(jnp.int32).astype(jnp.int16)
    for n, ref in enumerate(refs):
        for part in range(parts):
            ref[part * rows : (part + 1) * rows, :] = coded[
                n * rows : (n + 1) * rows, part * LANES : (part + 1) * LANES
            ]
        ref[parts * rows :, :] = scales


def decode(ref, cols):
    parts = cols // LANES
    rows = (ref.shape[0] - PAD) // parts
    power = ref[parts * rows :, :].astype(jnp.int32).astype(jnp.float32)
    scale = jnp.exp2(power * (1.0 / STEPS)) * (1.0 / LEVELS)
    return jnp.concatenate(
        [
            ref[part * rows : (part + 1) * rows, :].astype(jnp.int32).astype(jnp.float32)
            * scale[part : part + 1]
            for part in range(parts)
        ],
        axis=1,
    )


def mean_kernel(
    n_rep, n_y, n_f, key_hbm, act, grads, local, anchor, gathered, turned,
    key, proj, columns, weights, own_anchor, base, total, pg, grads_in, y_out, y_in, z_out, z_in,
    act_s, act_r, pg_s, pg_r, y1_s, y1_r, z1_s, z1_r, z2_s, z2_r, y2_s, y2_r, here,
):
    n_z = n_rep // n_y
    chunks, tokens_all, width = columns.shape
    tokens = tokens_all // n_f
    half = width // n_y
    block = half // n_z
    depth = weights.shape[2]
    rank = pg.shape[1]
    rep = lax.axis_index("replica")
    f = lax.axis_index("fsdp")
    z, y = rep // n_y, rep % n_y
    other = n_y - 1 - y
    y_peer = {"replica": z * n_y + other}

    def z_peer(d):
        return {"replica": ((z + d) % n_z) * n_y + y}

    barrier = pltpu.get_barrier_semaphore()
    for d in range(1, n_f):
        pl.semaphore_signal(barrier, inc=1, device_id={"fsdp": (f + d) % n_f}, device_id_type=MESH)
    for d in range(1, n_z):
        pl.semaphore_signal(barrier, inc=1, device_id=z_peer(d), device_id_type=MESH)
    pl.semaphore_signal(barrier, inc=1, device_id=y_peer, device_id_type=MESH)

    def remote(src, dst, send, recv, device):
        return pltpu.make_async_remote_copy(
            src_ref=src, dst_ref=dst, send_sem=send, recv_sem=recv,
            device_id=device, device_id_type=MESH,
        )

    mine = pl.ds(pl.multiple_of(f * tokens, tokens), tokens)

    def act_copy(c, d):
        g = (f + d) % n_f
        at = pl.ds(pl.multiple_of((g * chunks + c) * width, width), width)
        return remote(
            act.at[0, :, at], columns.at[c, mine, :], act_s.at[c, d - 1], act_r.at[c, d - 1],
            {"fsdp": g},
        )

    def act_own(c):
        at = pl.ds(pl.multiple_of((f * chunks + c) * width, width), width)
        return pltpu.make_async_copy(act.at[0, :, at], columns.at[c, mine, :], here.at[0, c])

    def weight_copy(c):
        at = pl.ds(pl.multiple_of(c * width, width), width)
        return pltpu.make_async_copy(local.at[0, at, :], weights.at[c], here.at[1, c])

    def anchor_copy(c):
        at = pl.ds(pl.multiple_of(c * width + y * half + z * block, block), block)
        return pltpu.make_async_copy(anchor.at[at, :], own_anchor.at[pl.ds(c * block, block), :], here.at[2, c])

    def pg_copy(d):
        return remote(
            pg.at[mine, :], pg.at[mine, :], pg_s.at[d - 1], pg_r.at[d - 1], {"fsdp": (f + d) % n_f}
        )

    def y1_copy(c):
        return remote(y_out.at[c], y_in.at[c], y1_s.at[c], y1_r.at[c], y_peer)

    def z1_copy(c, d):
        return remote(
            z_out.at[c, (z + d) % n_z], z_in.at[c, d - 1], z1_s.at[c, d - 1], z1_r.at[c, d - 1], z_peer(d)
        )

    def z2_copy(c, d):
        return remote(
            gathered.at[c, y, z], gathered.at[c, y, z], z2_s.at[c, d - 1], z2_r.at[c, d - 1],
            z_peer(d),
        )

    def y2_copy(c):
        return remote(gathered.at[c, y], gathered.at[c, y], y2_s.at[c], y2_r.at[c], y_peer)

    fetch = pltpu.make_async_copy(grads.at[0], grads_in, here.at[3, 0])
    fetch.start()
    words = pltpu.make_async_copy(key_hbm, key, here.at[3, 1])
    words.start()
    for c in range(chunks):
        weight_copy(c).start()
        act_own(c).start()
        anchor_copy(c).start()
    pl.semaphore_wait(barrier, n_f + n_z - 1)
    order = sorted(range(1, n_f), key=lambda d: abs(d - n_f // 2))
    for d in order:
        act_copy(0, d).start()
    words.wait()

    @pl.loop(0, depth, step=rank)
    def _(k):
        at = pl.ds(pl.multiple_of(k, rank), rank)
        high, low = split(projection(key[0], key[1], rank, rank, k))
        proj[at, :rank] = high
        proj[at, rank:] = low

    fetch.wait()
    both = dot(grads_in[...], proj[...])
    pg[mine, :] = (both[:, :rank] + both[:, rank:]).astype(jnp.bfloat16)
    for d in order:
        pg_copy(d).start()
    for c in range(1, min(AHEAD, chunks)):
        for d in order:
            act_copy(c, d).start()

    @pl.loop(0, chunks)
    def _(c):
        weight_copy(c).wait()
        both = dot(weights[c], proj[...])
        total[c] = (both[:, :rank] + both[:, rank:]) * (-1.0 / n_rep)

    for c in range(chunks):
        anchor_copy(c).wait()
    high, low = split(own_anchor[...])
    both = dot(high, proj[...])
    base[...] = both[:, :rank] + both[:, rank:] + dot(low, proj[:, :rank])

    for k in range(0, depth, rank):
        high, low = split(projection(key[0], key[1], rank, rank, k, True))
        turned[:rank, k : k + rank] = high
        turned[rank : 2 * rank, k : k + rank] = low
        turned[2 * rank :, k : k + rank] = high
    for d in range(1, n_f):
        pg_copy(d).wait_recv()
    scale = float(tokens_all) ** (-0.5) / n_rep

    def partial_sum(c):
        act_own(c).wait()
        for d in range(1, n_f):
            act_copy(c, d).wait_recv()

        @pl.when(c + AHEAD < chunks)
        def _():
            for d in order:
                act_copy(c + AHEAD, d).start()

        total[c] += dot(columns[c], pg[...], TN) * scale
        far = pl.ds(pl.multiple_of(other * half, half), half)
        encode(total[c, far, :], [y_out.at[c]])
        y1_copy(c).start()

    def sum_of_pair(c):
        y1_copy(c).wait_recv()
        near = pl.ds(pl.multiple_of(y * half, half), half)
        pair = total[c, near, :] + decode(y_in.at[c], rank)
        total[c, near, :] = pair
        encode(pair, [z_out.at[c, q] for q in range(n_z)])
        for d in range(1, n_z):
            z1_copy(c, d).start()

    def whole_mean(c):
        at = pl.ds(pl.multiple_of(y * half + z * block, block), block)
        own = pl.ds(pl.multiple_of(c * block, block), block)
        value = total[c, at, :] + base[own, :]
        for d in range(1, n_z):
            z1_copy(c, d).wait_recv()
            value += decode(z_in.at[c, d - 1], rank)
        encode(value, [gathered.at[c, y, z]])
        for d in range(1, n_z):
            z2_copy(c, d).start()

    def hand_over(c):
        for d in range(1, n_z):
            z2_copy(c, d).wait_recv()
        y2_copy(c).start()

    stages = ((partial_sum, 0), (hand_over, 4), (sum_of_pair, 1), (whole_mean, 2))

    @pl.loop(0, chunks + 4)
    def _(t):
        for stage, lag in stages:

            @pl.when(jnp.logical_and(t >= lag, t < chunks + lag))
            def _(stage=stage, lag=lag):
                stage(t - lag)

    for d in range(1, n_f):
        pg_copy(d).wait_send()

    @pl.loop(0, chunks)
    def _(c):
        for d in range(1, n_f):
            act_copy(c, d).wait_send()
        y1_copy(c).wait_send()
        for d in range(1, n_z):
            z1_copy(c, d).wait_send()
            z2_copy(c, d).wait_send()
        y2_copy(c).wait_send()
        y2_copy(c).wait_recv()


def update_kernel(
    gathered, turned, anchor, momentum, new_anchor, new_momentum, anchor_out, momentum_out, sems
):
    chunks, n_y, n_z = gathered.shape[:3]
    rank = momentum.shape[1]
    steps = chunks // GROUP
    width = momentum.shape[0] // steps

    def stores(c):
        at = pl.ds(pl.multiple_of(c * width, width), width)
        slot = c % 2
        return (
            pltpu.make_async_copy(anchor_out.at[slot], new_anchor.at[at, :], sems.at[0, slot]),
            pltpu.make_async_copy(momentum_out.at[slot], new_momentum.at[at, :], sems.at[1, slot]),
        )

    @pl.loop(0, steps)
    def _(c):
        slot = c % 2

        @pl.when(c >= 2)
        def _():
            for store in stores(c - 2):
                store.wait()

        mean = jnp.concatenate(
            [
                decode(gathered.at[c * GROUP + g, h, q], rank)
                for g in range(GROUP)
                for h in range(n_y)
                for q in range(n_z)
            ],
            axis=0,
        )
        at = pl.ds(pl.multiple_of(c * width, width), width)
        moved = 0.9 * momentum[at, :] + mean
        momentum_out[slot] = moved
        high, low = split(mean + 0.9 * moved)
        step = dot(jnp.concatenate([high, high, low], axis=1), turned[...])
        anchor_out[slot] = anchor[at, :] - 0.7 * step
        for store in stores(c):
            store.start()

    for c in range(max(steps - 2, 0), steps):
        for store in stores(c):
            store.wait()


def in_kernels(n_rep, n_y, n_f, act, grads, local, anchor, momentum, key):
    n_z = n_rep // n_y
    rows, depth = anchor.shape
    rank = momentum.shape[1]
    tokens = act.shape[1]
    width = rows // CHUNKS
    half = width // n_y
    block = half // n_z
    dma = pltpu.SemaphoreType.DMA
    hbm = pl.BlockSpec(memory_space=pltpu.HBM)
    coded = rank // LANES
    vmem = pl.BlockSpec(memory_space=pltpu.VMEM)
    gathered, turned = pl.pallas_call(
        functools.partial(mean_kernel, n_rep, n_y, n_f),
        out_shape=(
            jax.ShapeDtypeStruct((CHUNKS, n_y, n_z, coded * block + PAD, LANES), jnp.int16),
            jax.ShapeDtypeStruct((3 * rank, depth), jnp.bfloat16),
        ),
        in_specs=[hbm] * 5,
        out_specs=(vmem, vmem),
        scratch_shapes=[
            pltpu.SMEM(key.shape, jnp.int32),
            pltpu.VMEM((depth, 2 * rank), jnp.bfloat16),
            pltpu.VMEM((CHUNKS, tokens * n_f, width), jnp.bfloat16),
            pltpu.VMEM((CHUNKS, width, depth), jnp.bfloat16),
            pltpu.VMEM((CHUNKS * block, depth), jnp.float32),
            pltpu.VMEM((CHUNKS * block, rank), jnp.float32),
            pltpu.VMEM((CHUNKS, width, rank), jnp.float32),
            pltpu.VMEM((tokens * n_f, rank), jnp.bfloat16),
            pltpu.VMEM((tokens, depth), jnp.bfloat16),
            pltpu.VMEM((CHUNKS, coded * half + PAD, LANES), jnp.int16),
            pltpu.VMEM((CHUNKS, coded * half + PAD, LANES), jnp.int16),
            pltpu.VMEM((CHUNKS, n_z, coded * block + PAD, LANES), jnp.int16),
            pltpu.VMEM((CHUNKS, n_z - 1, coded * block + PAD, LANES), jnp.int16),
            dma((CHUNKS, n_f - 1)),
            dma((CHUNKS, n_f - 1)),
            dma((n_f - 1,)),
            dma((n_f - 1,)),
            dma((CHUNKS,)),
            dma((CHUNKS,)),
            dma((CHUNKS, n_z - 1)),
            dma((CHUNKS, n_z - 1)),
            dma((CHUNKS, n_z - 1)),
            dma((CHUNKS, n_z - 1)),
            dma((CHUNKS,)),
            dma((CHUNKS,)),
            dma((4, CHUNKS)),
        ],
        compiler_params=pltpu.CompilerParams(
            collective_id=0, has_side_effects=True, vmem_limit_bytes=51700 * 1024
        ),
        name="mean",
    )(key, act, grads, local, anchor)

    return pl.pallas_call(
        update_kernel,
        out_shape=(
            jax.ShapeDtypeStruct(anchor.shape, anchor.dtype),
            jax.ShapeDtypeStruct(momentum.shape, momentum.dtype),
        ),
        in_specs=[vmem] * 4,
        out_specs=(hbm, hbm),
        scratch_shapes=[
            pltpu.VMEM((2, GROUP * width, depth), jnp.float32),
            pltpu.VMEM((2, GROUP * width, rank), jnp.float32),
            dma((2, 2)),
        ],
        compiler_params=pltpu.CompilerParams(vmem_limit_bytes=32 * 1024 * 1024),
        name="update",
    )(gathered, turned, anchor, momentum)


def in_steps(activations, grad_out, local_weight, anchor, momentum, projection_key):
    inputs = activations[0]
    grads = grad_out[0]
    local = local_weight[0]
    proj = projection(projection_key[0], projection_key[1], grads.shape[1], momentum.shape[1])
    replicas = lax.axis_size("replica")
    scale = float(inputs.shape[0] * lax.axis_size("fsdp")) ** (-0.5)
    drift = anchor - local.astype(jnp.float32)
    columns = lax.all_to_all(inputs, "fsdp", split_axis=1, concat_axis=0, tiled=True)
    projected = jnp.dot(grads.astype(jnp.float32), proj, precision=HIGH)
    grad_part = lax.dot_general(
        columns.astype(jnp.float32),
        lax.all_gather(projected.astype(jnp.bfloat16), "fsdp", axis=0, tiled=True).astype(
            jnp.float32
        ),
        TN,
        precision=HIGH,
        preferred_element_type=jnp.float32,
    )
    local_term = jnp.dot(drift, proj, precision=HIGH) + scale * grad_part
    compressed_mean = lax.psum(local_term, "replica") / replicas
    new_momentum = 0.9 * momentum + compressed_mean
    update = compressed_mean + 0.9 * new_momentum
    new_anchor = anchor - 0.7 * jnp.dot(update, proj.T, precision=HIGH)
    return (new_anchor, new_momentum)


def solution(mesh):
    n_rep, n_f = mesh.shape["replica"], mesh.shape["fsdp"]
    n_y = 2

    def on_device(act, grads, local, anchor, momentum, key):
        rows, depth = anchor.shape
        rank = momentum.shape[1]
        fits = n_rep % n_y == 0 and n_rep > n_y and n_f > 1
        fits = fits and rows % (CHUNKS * n_rep * 16) == 0 and (rows // CHUNKS) % 128 == 0
        fits = fits and act.shape[1] % 16 == 0 and rank % 128 == 0 and depth % rank == 0
        if fits:
            return in_kernels(n_rep, n_y, n_f, act, grads, local, anchor, momentum, key)
        return in_steps(act, grads, local, anchor, momentum, key)

    placed = (
        P("replica", "fsdp", None),
        P("replica", "fsdp", None),
        P("replica", "fsdp", None),
        P("fsdp", None),
        P("fsdp", None),
        P(),
    )
    return jax.shard_map(
        on_device,
        mesh=mesh,
        in_specs=placed,
        out_specs=(P("fsdp", None), P("fsdp", None)),
        check_vma=False,
    )
```

```python
import functools

import jax
import jax.numpy as jnp
from jax import lax
from jax.experimental import pallas as pl
from jax.experimental.pallas import tpu as pltpu
from jax.sharding import PartitionSpec as P

HIGH = lax.Precision.HIGHEST
MESH = pl.DeviceIdType.MESH
CHUNKS = 8
AHEAD = 4
GROUP = 2
PAD = 16
LANES = 128
LEVELS = 32500.0
STEPS = 256.0
TN = (((0,), (0,)), ((), ()))


def projection(word0, word1, rows, cols, first=0, turned=False):
    shape = (cols, rows) if turned else (rows, cols)
    k_index = lax.broadcasted_iota(jnp.int32, shape, int(turned)) + first
    r_index = lax.broadcasted_iota(jnp.int32, shape, int(not turned))
    hashed = word0 + k_index * 668265261 + r_index * 374761393 + word1 * 1103515245
    hashed = jnp.bitwise_xor(hashed, lax.shift_right_logical(hashed, jnp.int32(15)))
    hashed = hashed * 739982445
    hashed = jnp.bitwise_xor(hashed, lax.shift_right_logical(hashed, jnp.int32(12)))
    hashed = hashed * 695938361
    hashed = jnp.bitwise_xor(hashed, lax.shift_right_logical(hashed, jnp.int32(15)))
    level = jnp.bitwise_and(lax.shift_right_logical(hashed, jnp.int32(8)), 65535).astype(
        jnp.float32
    )
    return ((level + 0.5) / 65536.0 - 0.5) * (12.0 / float(cols)) ** 0.5


def split(value):
    high = value.astype(jnp.bfloat16)
    return high, (value - high.astype(jnp.float32)).astype(jnp.bfloat16)


def dot(a, b, dims=(((1,), (0,)), ((), ()))):
    return lax.dot_general(a, b, dims, preferred_element_type=jnp.float32)


def encode(value, refs):
    cols = value.shape[1]
    parts, rows = cols // LANES, value.shape[0] // len(refs)
    top = jnp.max(jnp.abs(value), axis=0, keepdims=True)
    power = jnp.ceil(jnp.log(jnp.maximum(top, 1e-30)) * (STEPS * 1.4426950408889634))
    factor = jnp.exp2(power * (-1.0 / STEPS)) * LEVELS
    coded = jnp.round(value * factor).astype(jnp.int32).astype(jnp.int16)
    line = lax.broadcasted_iota(jnp.int32, (PAD, LANES), 0)
    scales = jnp.zeros((PAD, LANES), jnp.float32)
    for part in range(parts):
        scales = jnp.where(line == part, power[:, part * LANES : (part + 1) * LANES], scales)
    scales = scales.astype(jnp.int32).astype(jnp.int16)
    for n, ref in enumerate(refs):
        for part in range(parts):
            ref[part * rows : (part + 1) * rows, :] = coded[
                n * rows : (n + 1) * rows, part * LANES : (part + 1) * LANES
            ]
        ref[parts * rows :, :] = scales


def decode(ref, cols):
    parts = cols // LANES
    rows = (ref.shape[0] - PAD) // parts
    power = ref[parts * rows :, :].astype(jnp.int32).astype(jnp.float32)
    scale = jnp.exp2(power * (1.0 / STEPS)) * (1.0 / LEVELS)
    return jnp.concatenate(
        [
            ref[part * rows : (part + 1) * rows, :].astype(jnp.int32).astype(jnp.float32)
            * scale[part : part + 1]
            for part in range(parts)
        ],
        axis=1,
    )


def mean_kernel(
    n_rep, n_y, n_f, key_hbm, act, grads, local, anchor, gathered, turned,
    key, proj, columns, weights, own_anchor, base, total, pg, grads_in, y_out, y_in, z_out, z_in,
    act_s, act_r, pg_s, pg_r, y1_s, y1_r, z1_s, z1_r, z2_s, z2_r, y2_s, y2_r, here,
):
    n_z = n_rep // n_y
    chunks, tokens_all, width = columns.shape
    tokens = tokens_all // n_f
    half = width // n_y
    block = half // n_z
    depth = weights.shape[2]
    rank = pg.shape[1]
    rep = lax.axis_index("replica")
    f = lax.axis_index("fsdp")
    z, y = rep // n_y, rep % n_y
    other = n_y - 1 - y
    y_peer = {"replica": z * n_y + other}

    def z_peer(d):
        return {"replica": ((z + d) % n_z) * n_y + y}

    barrier = pltpu.get_barrier_semaphore()
    for d in range(1, n_f):
        pl.semaphore_signal(barrier, inc=1, device_id={"fsdp": (f + d) % n_f}, device_id_type=MESH)
    for d in range(1, n_z):
        pl.semaphore_signal(barrier, inc=1, device_id=z_peer(d), device_id_type=MESH)
    pl.semaphore_signal(barrier, inc=1, device_id=y_peer, device_id_type=MESH)

    def remote(src, dst, send, recv, device):
        return pltpu.make_async_remote_copy(
            src_ref=src, dst_ref=dst, send_sem=send, recv_sem=recv,
            device_id=device, device_id_type=MESH,
        )

    mine = pl.ds(pl.multiple_of(f * tokens, tokens), tokens)

    def act_copy(c, d):
        g = (f + d) % n_f
        at = pl.ds(pl.multiple_of((g * chunks + c) * width, width), width)
        return remote(
            act.at[0, :, at], columns.at[c, mine, :], act_s.at[c, d - 1], act_r.at[c, d - 1],
            {"fsdp": g},
        )

    def act_own(c):
        at = pl.ds(pl.multiple_of((f * chunks + c) * width, width), width)
        return pltpu.make_async_copy(act.at[0, :, at], columns.at[c, mine, :], here.at[0, c])

    def weight_copy(c):
        at = pl.ds(pl.multiple_of(c * width, width), width)
        return pltpu.make_async_copy(local.at[0, at, :], weights.at[c], here.at[1, c])

    def anchor_copy(c):
        at = pl.ds(pl.multiple_of(c * width + y * half + z * block, block), block)
        return pltpu.make_async_copy(anchor.at[at, :], own_anchor.at[pl.ds(c * block, block), :], here.at[2, c])

    def pg_copy(d):
        return remote(
            pg.at[mine, :], pg.at[mine, :], pg_s.at[d - 1], pg_r.at[d - 1], {"fsdp": (f + d) % n_f}
        )

    def y1_copy(c):
        return remote(y_out.at[c], y_in.at[c], y1_s.at[c], y1_r.at[c], y_peer)

    def z1_copy(c, d):
        return remote(
            z_out.at[c, (z + d) % n_z], z_in.at[c, d - 1], z1_s.at[c, d - 1], z1_r.at[c, d - 1], z_peer(d)
        )

    def z2_copy(c, d):
        return remote(
            gathered.at[c, y, z], gathered.at[c, y, z], z2_s.at[c, d - 1], z2_r.at[c, d - 1],
            z_peer(d),
        )

    def y2_copy(c):
        return remote(gathered.at[c, y], gathered.at[c, y], y2_s.at[c], y2_r.at[c], y_peer)

    fetch = pltpu.make_async_copy(grads.at[0], grads_in, here.at[3, 0])
    fetch.start()
    words = pltpu.make_async_copy(key_hbm, key, here.at[3, 1])
    words.start()
    for c in range(chunks):
        weight_copy(c).start()
        act_own(c).start()
        anchor_copy(c).start()
    pl.semaphore_wait(barrier, n_f + n_z - 1)
    order = sorted(range(1, n_f), key=lambda d: abs(d - n_f // 2))
    for d in order:
        act_copy(0, d).start()
    words.wait()

    @pl.loop(0, depth, step=rank)
    def _(k):
        at = pl.ds(pl.multiple_of(k, rank), rank)
        high, low = split(projection(key[0], key[1], rank, rank, k))
        proj[at, :rank] = high
        proj[at, rank:] = low

    fetch.wait()
    both = dot(grads_in[...], proj[...])
    pg[mine, :] = (both[:, :rank] + both[:, rank:]).astype(jnp.bfloat16)
    for d in order:
        pg_copy(d).start()
    for c in range(1, min(AHEAD, chunks)):
        for d in order:
            act_copy(c, d).start()

    @pl.loop(0, chunks)
    def _(c):
        weight_copy(c).wait()
        both = dot(weights[c], proj[...])
        total[c] = (both[:, :rank] + both[:, rank:]) * (-1.0 / n_rep)

    for c in range(chunks):
        anchor_copy(c).wait()
    high, low = split(own_anchor[...])
    both = dot(high, proj[...])
    base[...] = both[:, :rank] + both[:, rank:] + dot(low, proj[:, :rank])

    for k in range(0, depth, rank):
        high, low = split(projection(key[0], key[1], rank, rank, k, True))
        turned[:rank, k : k + rank] = high
        turned[rank : 2 * rank, k : k + rank] = low
        turned[2 * rank :, k : k + rank] = high
    for d in range(1, n_f):
        pg_copy(d).wait_recv()
    scale = float(tokens_all) ** (-0.5) / n_rep

    def partial_sum(c):
        act_own(c).wait()
        for d in range(1, n_f):
            act_copy(c, d).wait_recv()

        @pl.when(c + AHEAD < chunks)
        def _():
            for d in order:
                act_copy(c + AHEAD, d).start()

        total[c] += dot(columns[c], pg[...], TN) * scale
        far = pl.ds(pl.multiple_of(other * half, half), half)
        encode(total[c, far, :], [y_out.at[c]])
        y1_copy(c).start()

    def sum_of_pair(c):
        y1_copy(c).wait_recv()
        near = pl.ds(pl.multiple_of(y * half, half), half)
        pair = total[c, near, :] + decode(y_in.at[c], rank)
        total[c, near, :] = pair
        encode(pair, [z_out.at[c, q] for q in range(n_z)])
        for d in range(1, n_z):
            z1_copy(c, d).start()

    def whole_mean(c):
        at = pl.ds(pl.multiple_of(y * half + z * block, block), block)
        own = pl.ds(pl.multiple_of(c * block, block), block)
        value = total[c, at, :] + base[own, :]
        for d in range(1, n_z):
            z1_copy(c, d).wait_recv()
            value += decode(z_in.at[c, d - 1], rank)
        encode(value, [gathered.at[c, y, z]])
        for d in range(1, n_z):
            z2_copy(c, d).start()

    def hand_over(c):
        for d in range(1, n_z):
            z2_copy(c, d).wait_recv()
        y2_copy(c).start()

    stages = ((partial_sum, 0), (hand_over, 6), (whole_mean, 4), (sum_of_pair, 2))

    @pl.loop(0, chunks + 6)
    def _(t):
        for stage, lag in stages:

            @pl.when(jnp.logical_and(t >= lag, t < chunks + lag))
            def _(stage=stage, lag=lag):
                stage(t - lag)

    for d in range(1, n_f):
        pg_copy(d).wait_send()

    @pl.loop(0, chunks)
    def _(c):
        for d in range(1, n_f):
            act_copy(c, d).wait_send()
        y1_copy(c).wait_send()
        for d in range(1, n_z):
            z1_copy(c, d).wait_send()
            z2_copy(c, d).wait_send()
        y2_copy(c).wait_send()
        y2_copy(c).wait_recv()


def update_kernel(
    gathered, turned, anchor, momentum, new_anchor, new_momentum, anchor_out, momentum_out, sems
):
    chunks, n_y, n_z = gathered.shape[:3]
    rank = momentum.shape[1]
    steps = chunks // GROUP
    width = momentum.shape[0] // steps

    def stores(c):
        at = pl.ds(pl.multiple_of(c * width, width), width)
        slot = c % 2
        return (
            pltpu.make_async_copy(anchor_out.at[slot], new_anchor.at[at, :], sems.at[0, slot]),
            pltpu.make_async_copy(momentum_out.at[slot], new_momentum.at[at, :], sems.at[1, slot]),
        )

    @pl.loop(0, steps)
    def _(c):
        slot = c % 2

        @pl.when(c >= 2)
        def _():
            for store in stores(c - 2):
                store.wait()

        mean = jnp.concatenate(
            [
                decode(gathered.at[c * GROUP + g, h, q], rank)
                for g in range(GROUP)
                for h in range(n_y)
                for q in range(n_z)
            ],
            axis=0,
        )
        at = pl.ds(pl.multiple_of(c * width, width), width)
        moved = 0.9 * momentum[at, :] + mean
        momentum_out[slot] = moved
        high, low = split(mean + 0.9 * moved)
        step = dot(jnp.concatenate([high, high, low], axis=1), turned[...])
        anchor_out[slot] = anchor[at, :] - 0.7 * step
        for store in stores(c):
            store.start()

    for c in range(max(steps - 2, 0), steps):
        for store in stores(c):
            store.wait()


def in_kernels(n_rep, n_y, n_f, act, grads, local, anchor, momentum, key):
    n_z = n_rep // n_y
    rows, depth = anchor.shape
    rank = momentum.shape[1]
    tokens = act.shape[1]
    width = rows // CHUNKS
    half = width // n_y
    block = half // n_z
    dma = pltpu.SemaphoreType.DMA
    hbm = pl.BlockSpec(memory_space=pltpu.HBM)
    coded = rank // LANES
    vmem = pl.BlockSpec(memory_space=pltpu.VMEM)
    gathered, turned = pl.pallas_call(
        functools.partial(mean_kernel, n_rep, n_y, n_f),
        out_shape=(
            jax.ShapeDtypeStruct((CHUNKS, n_y, n_z, coded * block + PAD, LANES), jnp.int16),
            jax.ShapeDtypeStruct((3 * rank, depth), jnp.bfloat16),
        ),
        in_specs=[hbm] * 5,
        out_specs=(vmem, vmem),
        scratch_shapes=[
            pltpu.SMEM(key.shape, jnp.int32),
            pltpu.VMEM((depth, 2 * rank), jnp.bfloat16),
            pltpu.VMEM((CHUNKS, tokens * n_f, width), jnp.bfloat16),
            pltpu.VMEM((CHUNKS, width, depth), jnp.bfloat16),
            pltpu.VMEM((CHUNKS * block, depth), jnp.float32),
            pltpu.VMEM((CHUNKS * block, rank), jnp.float32),
            pltpu.VMEM((CHUNKS, width, rank), jnp.float32),
            pltpu.VMEM((tokens * n_f, rank), jnp.bfloat16),
            pltpu.VMEM((tokens, depth), jnp.bfloat16),
            pltpu.VMEM((CHUNKS, coded * half + PAD, LANES), jnp.int16),
            pltpu.VMEM((CHUNKS, coded * half + PAD, LANES), jnp.int16),
            pltpu.VMEM((CHUNKS, n_z, coded * block + PAD, LANES), jnp.int16),
            pltpu.VMEM((CHUNKS, n_z - 1, coded * block + PAD, LANES), jnp.int16),
            dma((CHUNKS, n_f - 1)),
            dma((CHUNKS, n_f - 1)),
            dma((n_f - 1,)),
            dma((n_f - 1,)),
            dma((CHUNKS,)),
            dma((CHUNKS,)),
            dma((CHUNKS, n_z - 1)),
            dma((CHUNKS, n_z - 1)),
            dma((CHUNKS, n_z - 1)),
            dma((CHUNKS, n_z - 1)),
            dma((CHUNKS,)),
            dma((CHUNKS,)),
            dma((4, CHUNKS)),
        ],
        compiler_params=pltpu.CompilerParams(
            collective_id=0, has_side_effects=True, vmem_limit_bytes=51700 * 1024
        ),
        name="mean",
    )(key, act, grads, local, anchor)

    return pl.pallas_call(
        update_kernel,
        out_shape=(
            jax.ShapeDtypeStruct(anchor.shape, anchor.dtype),
            jax.ShapeDtypeStruct(momentum.shape, momentum.dtype),
        ),
        in_specs=[vmem] * 4,
        out_specs=(hbm, hbm),
        scratch_shapes=[
            pltpu.VMEM((2, GROUP * width, depth), jnp.float32),
            pltpu.VMEM((2, GROUP * width, rank), jnp.float32),
            dma((2, 2)),
        ],
        compiler_params=pltpu.CompilerParams(vmem_limit_bytes=32 * 1024 * 1024),
        name="update",
    )(gathered, turned, anchor, momentum)


def in_steps(activations, grad_out, local_weight, anchor, momentum, projection_key):
    inputs = activations[0]
    grads = grad_out[0]
    local = local_weight[0]
    proj = projection(projection_key[0], projection_key[1], grads.shape[1], momentum.shape[1])
    replicas = lax.axis_size("replica")
    scale = float(inputs.shape[0] * lax.axis_size("fsdp")) ** (-0.5)
    drift = anchor - local.astype(jnp.float32)
    columns = lax.all_to_all(inputs, "fsdp", split_axis=1, concat_axis=0, tiled=True)
    projected = jnp.dot(grads.astype(jnp.float32), proj, precision=HIGH)
    grad_part = lax.dot_general(
        columns.astype(jnp.float32),
        lax.all_gather(projected.astype(jnp.bfloat16), "fsdp", axis=0, tiled=True).astype(
            jnp.float32
        ),
        TN,
        precision=HIGH,
        preferred_element_type=jnp.float32,
    )
    local_term = jnp.dot(drift, proj, precision=HIGH) + scale * grad_part
    compressed_mean = lax.psum(local_term, "replica") / replicas
    new_momentum = 0.9 * momentum + compressed_mean
    update = compressed_mean + 0.9 * new_momentum
    new_anchor = anchor - 0.7 * jnp.dot(update, proj.T, precision=HIGH)
    return (new_anchor, new_momentum)


def solution(mesh):
    n_rep, n_f = mesh.shape["replica"], mesh.shape["fsdp"]
    n_y = 2

    def on_device(act, grads, local, anchor, momentum, key):
        rows, depth = anchor.shape
        rank = momentum.shape[1]
        fits = n_rep % n_y == 0 and n_rep > n_y and n_f > 1
        fits = fits and rows % (CHUNKS * n_rep * 16) == 0 and (rows // CHUNKS) % 128 == 0
        fits = fits and act.shape[1] % 16 == 0 and rank % 128 == 0 and depth % rank == 0
        if fits:
            return in_kernels(n_rep, n_y, n_f, act, grads, local, anchor, momentum, key)
        return in_steps(act, grads, local, anchor, momentum, key)

    placed = (
        P("replica", "fsdp", None),
        P("replica", "fsdp", None),
        P("replica", "fsdp", None),
        P("fsdp", None),
        P("fsdp", None),
        P(),
    )
    return jax.shard_map(
        on_device,
        mesh=mesh,
        in_specs=placed,
        out_specs=(P("fsdp", None), P("fsdp", None)),
        check_vma=False,
    )
```

```python
import functools

import jax
import jax.numpy as jnp
from jax import lax
from jax.experimental import pallas as pl
from jax.experimental.pallas import tpu as pltpu
from jax.sharding import PartitionSpec as P

HIGH = lax.Precision.HIGHEST
MESH = pl.DeviceIdType.MESH
CHUNKS = 8
AHEAD = 3
GROUP = 2
PAD = 16
LANES = 128
LEVELS = 32500.0
STEPS = 256.0
TN = (((0,), (0,)), ((), ()))


def projection(word0, word1, rows, cols, first=0, turned=False):
    shape = (cols, rows) if turned else (rows, cols)
    k_index = lax.broadcasted_iota(jnp.int32, shape, int(turned)) + first
    r_index = lax.broadcasted_iota(jnp.int32, shape, int(not turned))
    hashed = word0 + k_index * 668265261 + r_index * 374761393 + word1 * 1103515245
    hashed = jnp.bitwise_xor(hashed, lax.shift_right_logical(hashed, jnp.int32(15)))
    hashed = hashed * 739982445
    hashed = jnp.bitwise_xor(hashed, lax.shift_right_logical(hashed, jnp.int32(12)))
    hashed = hashed * 695938361
    hashed = jnp.bitwise_xor(hashed, lax.shift_right_logical(hashed, jnp.int32(15)))
    level = jnp.bitwise_and(lax.shift_right_logical(hashed, jnp.int32(8)), 65535).astype(
        jnp.float32
    )
    return ((level + 0.5) / 65536.0 - 0.5) * (12.0 / float(cols)) ** 0.5


def split(value):
    high = value.astype(jnp.bfloat16)
    return high, (value - high.astype(jnp.float32)).astype(jnp.bfloat16)


def dot(a, b, dims=(((1,), (0,)), ((), ()))):
    return lax.dot_general(a, b, dims, preferred_element_type=jnp.float32)


def encode(value, refs):
    cols = value.shape[1]
    parts, rows = cols // LANES, value.shape[0] // len(refs)
    top = jnp.max(jnp.abs(value), axis=0, keepdims=True)
    power = jnp.ceil(jnp.log(jnp.maximum(top, 1e-30)) * (STEPS * 1.4426950408889634))
    factor = jnp.exp2(power * (-1.0 / STEPS)) * LEVELS
    coded = jnp.round(value * factor).astype(jnp.int32).astype(jnp.int16)
    line = lax.broadcasted_iota(jnp.int32, (PAD, LANES), 0)
    scales = jnp.zeros((PAD, LANES), jnp.float32)
    for part in range(parts):
        scales = jnp.where(line == part, power[:, part * LANES : (part + 1) * LANES], scales)
    scales = scales.astype(jnp.int32).astype(jnp.int16)
    for n, ref in enumerate(refs):
        for part in range(parts):
            ref[part * rows : (part + 1) * rows, :] = coded[
                n * rows : (n + 1) * rows, part * LANES : (part + 1) * LANES
            ]
        ref[parts * rows :, :] = scales


def decode(ref, cols):
    parts = cols // LANES
    rows = (ref.shape[0] - PAD) // parts
    power = ref[parts * rows :, :].astype(jnp.int32).astype(jnp.float32)
    scale = jnp.exp2(power * (1.0 / STEPS)) * (1.0 / LEVELS)
    return jnp.concatenate(
        [
            ref[part * rows : (part + 1) * rows, :].astype(jnp.int32).astype(jnp.float32)
            * scale[part : part + 1]
            for part in range(parts)
        ],
        axis=1,
    )


def mean_kernel(
    n_rep, n_y, n_f, key_hbm, act, grads, local, anchor, gathered, turned,
    key, proj, columns, weights, own_anchor, base, total, pg, grads_in, y_out, y_in, z_out, z_in,
    act_s, act_r, pg_s, pg_r, y1_s, y1_r, z1_s, z1_r, z2_s, z2_r, y2_s, y2_r, here,
):
    n_z = n_rep // n_y
    chunks, tokens_all, width = columns.shape
    tokens = tokens_all // n_f
    half = width // n_y
    block = half // n_z
    depth = weights.shape[2]
    rank = pg.shape[1]
    rep = lax.axis_index("replica")
    f = lax.axis_index("fsdp")
    z, y = rep // n_y, rep % n_y
    other = n_y - 1 - y
    y_peer = {"replica": z * n_y + other}

    def z_peer(d):
        return {"replica": ((z + d) % n_z) * n_y + y}

    barrier = pltpu.get_barrier_semaphore()
    for d in range(1, n_f):
        pl.semaphore_signal(barrier, inc=1, device_id={"fsdp": (f + d) % n_f}, device_id_type=MESH)
    for d in range(1, n_z):
        pl.semaphore_signal(barrier, inc=1, device_id=z_peer(d), device_id_type=MESH)
    pl.semaphore_signal(barrier, inc=1, device_id=y_peer, device_id_type=MESH)

    def remote(src, dst, send, recv, device):
        return pltpu.make_async_remote_copy(
            src_ref=src, dst_ref=dst, send_sem=send, recv_sem=recv,
            device_id=device, device_id_type=MESH,
        )

    mine = pl.ds(pl.multiple_of(f * tokens, tokens), tokens)

    def act_copy(c, d):
        g = (f + d) % n_f
        at = pl.ds(pl.multiple_of((g * chunks + c) * width, width), width)
        return remote(
            act.at[0, :, at], columns.at[c, mine, :], act_s.at[c, d - 1], act_r.at[c, d - 1],
            {"fsdp": g},
        )

    def act_own(c):
        at = pl.ds(pl.multiple_of((f * chunks + c) * width, width), width)
        return pltpu.make_async_copy(act.at[0, :, at], columns.at[c, mine, :], here.at[0, c])

    def weight_copy(c):
        at = pl.ds(pl.multiple_of(c * width, width), width)
        return pltpu.make_async_copy(local.at[0, at, :], weights.at[c], here.at[1, c])

    def anchor_copy(c):
        at = pl.ds(pl.multiple_of(c * width + y * half + z * block, block), block)
        return pltpu.make_async_copy(anchor.at[at, :], own_anchor.at[pl.ds(c * block, block), :], here.at[2, c])

    def pg_copy(d):
        return remote(
            pg.at[mine, :], pg.at[mine, :], pg_s.at[d - 1], pg_r.at[d - 1], {"fsdp": (f + d) % n_f}
        )

    def y1_copy(c):
        return remote(y_out.at[c], y_in.at[c], y1_s.at[c], y1_r.at[c], y_peer)

    def z1_copy(c, d):
        return remote(
            z_out.at[c, (z + d) % n_z], z_in.at[c, d - 1], z1_s.at[c, d - 1], z1_r.at[c, d - 1], z_peer(d)
        )

    def z2_copy(c, d):
        return remote(
            gathered.at[c, y, z], gathered.at[c, y, z], z2_s.at[c, d - 1], z2_r.at[c, d - 1],
            z_peer(d),
        )

    def y2_copy(c):
        return remote(gathered.at[c, y], gathered.at[c, y], y2_s.at[c], y2_r.at[c], y_peer)

    fetch = pltpu.make_async_copy(grads.at[0], grads_in, here.at[3, 0])
    fetch.start()
    words = pltpu.make_async_copy(key_hbm, key, here.at[3, 1])
    words.start()
    for c in range(chunks):
        weight_copy(c).start()
        act_own(c).start()
        anchor_copy(c).start()
    pl.semaphore_wait(barrier, n_f + n_z - 1)
    order = sorted(range(1, n_f), key=lambda d: abs(d - n_f // 2))
    for d in order:
        act_copy(0, d).start()
    words.wait()

    @pl.loop(0, depth, step=rank)
    def _(k):
        at = pl.ds(pl.multiple_of(k, rank), rank)
        high, low = split(projection(key[0], key[1], rank, rank, k))
        proj[at, :rank] = high
        proj[at, rank:] = low

    fetch.wait()
    both = dot(grads_in[...], proj[...])
    pg[mine, :] = (both[:, :rank] + both[:, rank:]).astype(jnp.bfloat16)
    for d in order:
        pg_copy(d).start()
    for c in range(1, min(AHEAD, chunks)):
        for d in order:
            act_copy(c, d).start()

    @pl.loop(0, chunks)
    def _(c):
        weight_copy(c).wait()
        both = dot(weights[c], proj[...])
        total[c] = (both[:, :rank] + both[:, rank:]) * (-1.0 / n_rep)

    for c in range(chunks):
        anchor_copy(c).wait()
    high, low = split(own_anchor[...])
    both = dot(high, proj[...])
    base[...] = both[:, :rank] + both[:, rank:] + dot(low, proj[:, :rank])

    for k in range(0, depth, rank):
        high, low = split(projection(key[0], key[1], rank, rank, k, True))
        turned[:rank, k : k + rank] = high
        turned[rank : 2 * rank, k : k + rank] = low
        turned[2 * rank :, k : k + rank] = high
    for d in range(1, n_f):
        pg_copy(d).wait_recv()
    scale = float(tokens_all) ** (-0.5) / n_rep

    def partial_sum(c):
        act_own(c).wait()
        for d in range(1, n_f):
            act_copy(c, d).wait_recv()

        @pl.when(c + AHEAD < chunks)
        def _():
            for d in order:
                act_copy(c + AHEAD, d).start()

        total[c] += dot(columns[c], pg[...], TN) * scale
        far = pl.ds(pl.multiple_of(other * half, half), half)
        encode(total[c, far, :], [y_out.at[c]])
        y1_copy(c).start()

    def sum_of_pair(c):
        y1_copy(c).wait_recv()
        near = pl.ds(pl.multiple_of(y * half, half), half)
        pair = total[c, near, :] + decode(y_in.at[c], rank)
        total[c, near, :] = pair
        encode(pair, [z_out.at[c, q] for q in range(n_z)])
        for d in range(1, n_z):
            z1_copy(c, d).start()

    def whole_mean(c):
        at = pl.ds(pl.multiple_of(y * half + z * block, block), block)
        own = pl.ds(pl.multiple_of(c * block, block), block)
        value = total[c, at, :] + base[own, :]
        for d in range(1, n_z):
            z1_copy(c, d).wait_recv()
            value += decode(z_in.at[c, d - 1], rank)
        encode(value, [gathered.at[c, y, z]])
        for d in range(1, n_z):
            z2_copy(c, d).start()

    def hand_over(c):
        for d in range(1, n_z):
            z2_copy(c, d).wait_recv()
        y2_copy(c).start()

    stages = ((partial_sum, 0), (hand_over, 2), (whole_mean, 1), (sum_of_pair, 0))

    @pl.loop(0, chunks + 2)
    def _(t):
        for stage, lag in stages:

            @pl.when(jnp.logical_and(t >= lag, t < chunks + lag))
            def _(stage=stage, lag=lag):
                stage(t - lag)

    for d in range(1, n_f):
        pg_copy(d).wait_send()

    @pl.loop(0, chunks)
    def _(c):
        for d in range(1, n_f):
            act_copy(c, d).wait_send()
        y1_copy(c).wait_send()
        for d in range(1, n_z):
            z1_copy(c, d).wait_send()
            z2_copy(c, d).wait_send()
        y2_copy(c).wait_send()
        y2_copy(c).wait_recv()


def update_kernel(
    gathered, turned, anchor, momentum, new_anchor, new_momentum, anchor_out, momentum_out, sems
):
    chunks, n_y, n_z = gathered.shape[:3]
    rank = momentum.shape[1]
    steps = chunks // GROUP
    width = momentum.shape[0] // steps

    def stores(c):
        at = pl.ds(pl.multiple_of(c * width, width), width)
        slot = c % 2
        return (
            pltpu.make_async_copy(anchor_out.at[slot], new_anchor.at[at, :], sems.at[0, slot]),
            pltpu.make_async_copy(momentum_out.at[slot], new_momentum.at[at, :], sems.at[1, slot]),
        )

    @pl.loop(0, steps)
    def _(c):
        slot = c % 2

        @pl.when(c >= 2)
        def _():
            for store in stores(c - 2):
                store.wait()

        mean = jnp.concatenate(
            [
                decode(gathered.at[c * GROUP + g, h, q], rank)
                for g in range(GROUP)
                for h in range(n_y)
                for q in range(n_z)
            ],
            axis=0,
        )
        at = pl.ds(pl.multiple_of(c * width, width), width)
        moved = 0.9 * momentum[at, :] + mean
        momentum_out[slot] = moved
        high, low = split(mean + 0.9 * moved)
        step = dot(jnp.concatenate([high, high, low], axis=1), turned[...])
        anchor_out[slot] = anchor[at, :] - 0.7 * step
        for store in stores(c):
            store.start()

    for c in range(max(steps - 2, 0), steps):
        for store in stores(c):
            store.wait()


def in_kernels(n_rep, n_y, n_f, act, grads, local, anchor, momentum, key):
    n_z = n_rep // n_y
    rows, depth = anchor.shape
    rank = momentum.shape[1]
    tokens = act.shape[1]
    width = rows // CHUNKS
    half = width // n_y
    block = half // n_z
    dma = pltpu.SemaphoreType.DMA
    hbm = pl.BlockSpec(memory_space=pltpu.HBM)
    coded = rank // LANES
    vmem = pl.BlockSpec(memory_space=pltpu.VMEM)
    gathered, turned = pl.pallas_call(
        functools.partial(mean_kernel, n_rep, n_y, n_f),
        out_shape=(
            jax.ShapeDtypeStruct((CHUNKS, n_y, n_z, coded * block + PAD, LANES), jnp.int16),
            jax.ShapeDtypeStruct((3 * rank, depth), jnp.bfloat16),
        ),
        in_specs=[hbm] * 5,
        out_specs=(vmem, vmem),
        scratch_shapes=[
            pltpu.SMEM(key.shape, jnp.int32),
            pltpu.VMEM((depth, 2 * rank), jnp.bfloat16),
            pltpu.VMEM((CHUNKS, tokens * n_f, width), jnp.bfloat16),
            pltpu.VMEM((CHUNKS, width, depth), jnp.bfloat16),
            pltpu.VMEM((CHUNKS * block, depth), jnp.float32),
            pltpu.VMEM((CHUNKS * block, rank), jnp.float32),
            pltpu.VMEM((CHUNKS, width, rank), jnp.float32),
            pltpu.VMEM((tokens * n_f, rank), jnp.bfloat16),
            pltpu.VMEM((tokens, depth), jnp.bfloat16),
            pltpu.VMEM((CHUNKS, coded * half + PAD, LANES), jnp.int16),
            pltpu.VMEM((CHUNKS, coded * half + PAD, LANES), jnp.int16),
            pltpu.VMEM((CHUNKS, n_z, coded * block + PAD, LANES), jnp.int16),
            pltpu.VMEM((CHUNKS, n_z - 1, coded * block + PAD, LANES), jnp.int16),
            dma((CHUNKS, n_f - 1)),
            dma((CHUNKS, n_f - 1)),
            dma((n_f - 1,)),
            dma((n_f - 1,)),
            dma((CHUNKS,)),
            dma((CHUNKS,)),
            dma((CHUNKS, n_z - 1)),
            dma((CHUNKS, n_z - 1)),
            dma((CHUNKS, n_z - 1)),
            dma((CHUNKS, n_z - 1)),
            dma((CHUNKS,)),
            dma((CHUNKS,)),
            dma((4, CHUNKS)),
        ],
        compiler_params=pltpu.CompilerParams(
            collective_id=0, has_side_effects=True, vmem_limit_bytes=51700 * 1024
        ),
        name="mean",
    )(key, act, grads, local, anchor)

    return pl.pallas_call(
        update_kernel,
        out_shape=(
            jax.ShapeDtypeStruct(anchor.shape, anchor.dtype),
            jax.ShapeDtypeStruct(momentum.shape, momentum.dtype),
        ),
        in_specs=[vmem] * 4,
        out_specs=(hbm, hbm),
        scratch_shapes=[
            pltpu.VMEM((2, GROUP * width, depth), jnp.float32),
            pltpu.VMEM((2, GROUP * width, rank), jnp.float32),
            dma((2, 2)),
        ],
        compiler_params=pltpu.CompilerParams(vmem_limit_bytes=32 * 1024 * 1024),
        name="update",
    )(gathered, turned, anchor, momentum)


def in_steps(activations, grad_out, local_weight, anchor, momentum, projection_key):
    inputs = activations[0]
    grads = grad_out[0]
    local = local_weight[0]
    proj = projection(projection_key[0], projection_key[1], grads.shape[1], momentum.shape[1])
    replicas = lax.axis_size("replica")
    scale = float(inputs.shape[0] * lax.axis_size("fsdp")) ** (-0.5)
    drift = anchor - local.astype(jnp.float32)
    columns = lax.all_to_all(inputs, "fsdp", split_axis=1, concat_axis=0, tiled=True)
    projected = jnp.dot(grads.astype(jnp.float32), proj, precision=HIGH)
    grad_part = lax.dot_general(
        columns.astype(jnp.float32),
        lax.all_gather(projected.astype(jnp.bfloat16), "fsdp", axis=0, tiled=True).astype(
            jnp.float32
        ),
        TN,
        precision=HIGH,
        preferred_element_type=jnp.float32,
    )
    local_term = jnp.dot(drift, proj, precision=HIGH) + scale * grad_part
    compressed_mean = lax.psum(local_term, "replica") / replicas
    new_momentum = 0.9 * momentum + compressed_mean
    update = compressed_mean + 0.9 * new_momentum
    new_anchor = anchor - 0.7 * jnp.dot(update, proj.T, precision=HIGH)
    return (new_anchor, new_momentum)


def solution(mesh):
    n_rep, n_f = mesh.shape["replica"], mesh.shape["fsdp"]
    n_y = 2

    def on_device(act, grads, local, anchor, momentum, key):
        rows, depth = anchor.shape
        rank = momentum.shape[1]
        fits = n_rep % n_y == 0 and n_rep > n_y and n_f > 1
        fits = fits and rows % (CHUNKS * n_rep * 16) == 0 and (rows // CHUNKS) % 128 == 0
        fits = fits and act.shape[1] % 16 == 0 and rank % 128 == 0 and depth % rank == 0
        if fits:
            return in_kernels(n_rep, n_y, n_f, act, grads, local, anchor, momentum, key)
        return in_steps(act, grads, local, anchor, momentum, key)

    placed = (
        P("replica", "fsdp", None),
        P("replica", "fsdp", None),
        P("replica", "fsdp", None),
        P("fsdp", None),
        P("fsdp", None),
        P(),
    )
    return jax.shard_map(
        on_device,
        mesh=mesh,
        in_specs=placed,
        out_specs=(P("fsdp", None), P("fsdp", None)),
        check_vma=False,
    )
```

```python
import functools

import jax
import jax.numpy as jnp
from jax import lax
from jax.experimental import pallas as pl
from jax.experimental.pallas import tpu as pltpu
from jax.sharding import PartitionSpec as P

HIGH = lax.Precision.HIGHEST
MESH = pl.DeviceIdType.MESH
CHUNKS = 8
AHEAD = 2
GROUP = 2
PAD = 16
LANES = 128
LEVELS = 32500.0
STEPS = 256.0
TN = (((0,), (0,)), ((), ()))


def projection(word0, word1, rows, cols, first=0, turned=False):
    shape = (cols, rows) if turned else (rows, cols)
    k_index = lax.broadcasted_iota(jnp.int32, shape, int(turned)) + first
    r_index = lax.broadcasted_iota(jnp.int32, shape, int(not turned))
    hashed = word0 + k_index * 668265261 + r_index * 374761393 + word1 * 1103515245
    hashed = jnp.bitwise_xor(hashed, lax.shift_right_logical(hashed, jnp.int32(15)))
    hashed = hashed * 739982445
    hashed = jnp.bitwise_xor(hashed, lax.shift_right_logical(hashed, jnp.int32(12)))
    hashed = hashed * 695938361
    hashed = jnp.bitwise_xor(hashed, lax.shift_right_logical(hashed, jnp.int32(15)))
    level = jnp.bitwise_and(lax.shift_right_logical(hashed, jnp.int32(8)), 65535).astype(
        jnp.float32
    )
    return ((level + 0.5) / 65536.0 - 0.5) * (12.0 / float(cols)) ** 0.5


def split(value):
    high = value.astype(jnp.bfloat16)
    return high, (value - high.astype(jnp.float32)).astype(jnp.bfloat16)


def dot(a, b, dims=(((1,), (0,)), ((), ()))):
    return lax.dot_general(a, b, dims, preferred_element_type=jnp.float32)


def encode(value, refs):
    cols = value.shape[1]
    parts, rows = cols // LANES, value.shape[0] // len(refs)
    top = jnp.max(jnp.abs(value), axis=0, keepdims=True)
    power = jnp.ceil(jnp.log(jnp.maximum(top, 1e-30)) * (STEPS * 1.4426950408889634))
    factor = jnp.exp2(power * (-1.0 / STEPS)) * LEVELS
    coded = jnp.round(value * factor).astype(jnp.int32).astype(jnp.int16)
    line = lax.broadcasted_iota(jnp.int32, (PAD, LANES), 0)
    scales = jnp.zeros((PAD, LANES), jnp.float32)
    for part in range(parts):
        scales = jnp.where(line == part, power[:, part * LANES : (part + 1) * LANES], scales)
    scales = scales.astype(jnp.int32).astype(jnp.int16)
    for n, ref in enumerate(refs):
        for part in range(parts):
            ref[part * rows : (part + 1) * rows, :] = coded[
                n * rows : (n + 1) * rows, part * LANES : (part + 1) * LANES
            ]
        ref[parts * rows :, :] = scales


def decode(ref, cols):
    parts = cols // LANES
    rows = (ref.shape[0] - PAD) // parts
    power = ref[parts * rows :, :].astype(jnp.int32).astype(jnp.float32)
    scale = jnp.exp2(power * (1.0 / STEPS)) * (1.0 / LEVELS)
    return jnp.concatenate(
        [
            ref[part * rows : (part + 1) * rows, :].astype(jnp.int32).astype(jnp.float32)
            * scale[part : part + 1]
            for part in range(parts)
        ],
        axis=1,
    )


def mean_kernel(
    n_rep, n_y, n_f, key_hbm, act, grads, local, anchor, gathered, turned,
    key, proj, columns, weights, own_anchor, base, total, pg, grads_in, y_out, y_in, z_out, z_in,
    act_s, act_r, pg_s, pg_r, y1_s, y1_r, z1_s, z1_r, z2_s, z2_r, y2_s, y2_r, here,
):
    n_z = n_rep // n_y
    chunks, tokens_all, width = columns.shape
    tokens = tokens_all // n_f
    half = width // n_y
    block = half // n_z
    depth = weights.shape[2]
    rank = pg.shape[1]
    rep = lax.axis_index("replica")
    f = lax.axis_index("fsdp")
    z, y = rep // n_y, rep % n_y
    other = n_y - 1 - y
    y_peer = {"replica": z * n_y + other}

    def z_peer(d):
        return {"replica": ((z + d) % n_z) * n_y + y}

    barrier = pltpu.get_barrier_semaphore()
    for d in range(1, n_f):
        pl.semaphore_signal(barrier, inc=1, device_id={"fsdp": (f + d) % n_f}, device_id_type=MESH)
    for d in range(1, n_z):
        pl.semaphore_signal(barrier, inc=1, device_id=z_peer(d), device_id_type=MESH)
    pl.semaphore_signal(barrier, inc=1, device_id=y_peer, device_id_type=MESH)

    def remote(src, dst, send, recv, device):
        return pltpu.make_async_remote_copy(
            src_ref=src, dst_ref=dst, send_sem=send, recv_sem=recv,
            device_id=device, device_id_type=MESH,
        )

    mine = pl.ds(pl.multiple_of(f * tokens, tokens), tokens)

    def act_copy(c, d):
        g = (f + d) % n_f
        at = pl.ds(pl.multiple_of((g * chunks + c) * width, width), width)
        return remote(
            act.at[0, :, at], columns.at[c, mine, :], act_s.at[c, d - 1], act_r.at[c, d - 1],
            {"fsdp": g},
        )

    def act_own(c):
        at = pl.ds(pl.multiple_of((f * chunks + c) * width, width), width)
        return pltpu.make_async_copy(act.at[0, :, at], columns.at[c, mine, :], here.at[0, c])

    def weight_copy(c):
        at = pl.ds(pl.multiple_of(c * width, width), width)
        return pltpu.make_async_copy(local.at[0, at, :], weights.at[c], here.at[1, c])

    def anchor_copy(c):
        at = pl.ds(pl.multiple_of(c * width + y * half + z * block, block), block)
        return pltpu.make_async_copy(anchor.at[at, :], own_anchor.at[pl.ds(c * block, block), :], here.at[2, c])

    def pg_copy(d):
        return remote(
            pg.at[mine, :], pg.at[mine, :], pg_s.at[d - 1], pg_r.at[d - 1], {"fsdp": (f + d) % n_f}
        )

    def y1_copy(c):
        return remote(y_out.at[c], y_in.at[c], y1_s.at[c], y1_r.at[c], y_peer)

    def z1_copy(c, d):
        return remote(
            z_out.at[c, (z + d) % n_z], z_in.at[c, d - 1], z1_s.at[c, d - 1], z1_r.at[c, d - 1], z_peer(d)
        )

    def z2_copy(c, d):
        return remote(
            gathered.at[c, y, z], gathered.at[c, y, z], z2_s.at[c, d - 1], z2_r.at[c, d - 1],
            z_peer(d),
        )

    def y2_copy(c):
        return remote(gathered.at[c, y], gathered.at[c, y], y2_s.at[c], y2_r.at[c], y_peer)

    fetch = pltpu.make_async_copy(grads.at[0], grads_in, here.at[3, 0])
    fetch.start()
    words = pltpu.make_async_copy(key_hbm, key, here.at[3, 1])
    words.start()
    for c in range(chunks):
        weight_copy(c).start()
        act_own(c).start()
        anchor_copy(c).start()
    pl.semaphore_wait(barrier, n_f + n_z - 1)
    order = sorted(range(1, n_f), key=lambda d: abs(d - n_f // 2))
    for d in order:
        act_copy(0, d).start()
    words.wait()

    @pl.loop(0, depth, step=rank)
    def _(k):
        at = pl.ds(pl.multiple_of(k, rank), rank)
        high, low = split(projection(key[0], key[1], rank, rank, k))
        proj[at, :rank] = high
        proj[at, rank:] = low

    fetch.wait()
    both = dot(grads_in[...], proj[...])
    pg[mine, :] = (both[:, :rank] + both[:, rank:]).astype(jnp.bfloat16)
    for d in order:
        pg_copy(d).start()
    for c in range(1, min(AHEAD, chunks)):
        for d in order:
            act_copy(c, d).start()

    @pl.loop(0, chunks)
    def _(c):
        weight_copy(c).wait()
        both = dot(weights[c], proj[...])
        total[c] = (both[:, :rank] + both[:, rank:]) * (-1.0 / n_rep)

    for c in range(chunks):
        anchor_copy(c).wait()
    high, low = split(own_anchor[...])
    both = dot(high, proj[...])
    base[...] = both[:, :rank] + both[:, rank:] + dot(low, proj[:, :rank])

    for k in range(0, depth, rank):
        high, low = split(projection(key[0], key[1], rank, rank, k, True))
        turned[:rank, k : k + rank] = high
        turned[rank : 2 * rank, k : k + rank] = low
        turned[2 * rank :, k : k + rank] = high
    for d in range(1, n_f):
        pg_copy(d).wait_recv()
    scale = float(tokens_all) ** (-0.5) / n_rep

    def partial_sum(c):
        act_own(c).wait()
        for d in range(1, n_f):
            act_copy(c, d).wait_recv()

        total[c] += dot(columns[c], pg[...], TN) * scale
        far = pl.ds(pl.multiple_of(other * half, half), half)
        encode(total[c, far, :], [y_out.at[c]])
        y1_copy(c).start()

        @pl.when(c + AHEAD < chunks)
        def _():
            for d in order:
                act_copy(c + AHEAD, d).start()

    def sum_of_pair(c):
        y1_copy(c).wait_recv()
        near = pl.ds(pl.multiple_of(y * half, half), half)
        pair = total[c, near, :] + decode(y_in.at[c], rank)
        total[c, near, :] = pair
        encode(pair, [z_out.at[c, q] for q in range(n_z)])
        for d in range(1, n_z):
            z1_copy(c, d).start()

    def whole_mean(c):
        at = pl.ds(pl.multiple_of(y * half + z * block, block), block)
        own = pl.ds(pl.multiple_of(c * block, block), block)
        value = total[c, at, :] + base[own, :]
        for d in range(1, n_z):
            z1_copy(c, d).wait_recv()
            value += decode(z_in.at[c, d - 1], rank)
        encode(value, [gathered.at[c, y, z]])
        for d in range(1, n_z):
            z2_copy(c, d).start()

    def hand_over(c):
        for d in range(1, n_z):
            z2_copy(c, d).wait_recv()
        y2_copy(c).start()

    stages = ((partial_sum, 0), (hand_over, 4), (sum_of_pair, 1), (whole_mean, 2))

    @pl.loop(0, chunks + 4)
    def _(t):
        for stage, lag in stages:

            @pl.when(jnp.logical_and(t >= lag, t < chunks + lag))
            def _(stage=stage, lag=lag):
                stage(t - lag)

    for d in range(1, n_f):
        pg_copy(d).wait_send()

    @pl.loop(0, chunks)
    def _(c):
        for d in range(1, n_f):
            act_copy(c, d).wait_send()
        y1_copy(c).wait_send()
        for d in range(1, n_z):
            z1_copy(c, d).wait_send()
            z2_copy(c, d).wait_send()
        y2_copy(c).wait_send()
        y2_copy(c).wait_recv()


def update_kernel(
    gathered, turned, anchor, momentum, new_anchor, new_momentum, anchor_out, momentum_out, sems
):
    chunks, n_y, n_z = gathered.shape[:3]
    rank = momentum.shape[1]
    steps = chunks // GROUP
    width = momentum.shape[0] // steps

    def stores(c):
        at = pl.ds(pl.multiple_of(c * width, width), width)
        slot = c % 2
        return (
            pltpu.make_async_copy(anchor_out.at[slot], new_anchor.at[at, :], sems.at[0, slot]),
            pltpu.make_async_copy(momentum_out.at[slot], new_momentum.at[at, :], sems.at[1, slot]),
        )

    @pl.loop(0, steps)
    def _(c):
        slot = c % 2

        @pl.when(c >= 2)
        def _():
            for store in stores(c - 2):
                store.wait()

        mean = jnp.concatenate(
            [
                decode(gathered.at[c * GROUP + g, h, q], rank)
                for g in range(GROUP)
                for h in range(n_y)
                for q in range(n_z)
            ],
            axis=0,
        )
        at = pl.ds(pl.multiple_of(c * width, width), width)
        moved = 0.9 * momentum[at, :] + mean
        momentum_out[slot] = moved
        high, low = split(mean + 0.9 * moved)
        step = dot(jnp.concatenate([high, high, low], axis=1), turned[...])
        anchor_out[slot] = anchor[at, :] - 0.7 * step
        for store in stores(c):
            store.start()

    for c in range(max(steps - 2, 0), steps):
        for store in stores(c):
            store.wait()


def in_kernels(n_rep, n_y, n_f, act, grads, local, anchor, momentum, key):
    n_z = n_rep // n_y
    rows, depth = anchor.shape
    rank = momentum.shape[1]
    tokens = act.shape[1]
    width = rows // CHUNKS
    half = width // n_y
    block = half // n_z
    dma = pltpu.SemaphoreType.DMA
    hbm = pl.BlockSpec(memory_space=pltpu.HBM)
    coded = rank // LANES
    vmem = pl.BlockSpec(memory_space=pltpu.VMEM)
    gathered, turned = pl.pallas_call(
        functools.partial(mean_kernel, n_rep, n_y, n_f),
        out_shape=(
            jax.ShapeDtypeStruct((CHUNKS, n_y, n_z, coded * block + PAD, LANES), jnp.int16),
            jax.ShapeDtypeStruct((3 * rank, depth), jnp.bfloat16),
        ),
        in_specs=[hbm] * 5,
        out_specs=(vmem, vmem),
        scratch_shapes=[
            pltpu.SMEM(key.shape, jnp.int32),
            pltpu.VMEM((depth, 2 * rank), jnp.bfloat16),
            pltpu.VMEM((CHUNKS, tokens * n_f, width), jnp.bfloat16),
            pltpu.VMEM((CHUNKS, width, depth), jnp.bfloat16),
            pltpu.VMEM((CHUNKS * block, depth), jnp.float32),
            pltpu.VMEM((CHUNKS * block, rank), jnp.float32),
            pltpu.VMEM((CHUNKS, width, rank), jnp.float32),
            pltpu.VMEM((tokens * n_f, rank), jnp.bfloat16),
            pltpu.VMEM((tokens, depth), jnp.bfloat16),
            pltpu.VMEM((CHUNKS, coded * half + PAD, LANES), jnp.int16),
            pltpu.VMEM((CHUNKS, coded * half + PAD, LANES), jnp.int16),
            pltpu.VMEM((CHUNKS, n_z, coded * block + PAD, LANES), jnp.int16),
            pltpu.VMEM((CHUNKS, n_z - 1, coded * block + PAD, LANES), jnp.int16),
            dma((CHUNKS, n_f - 1)),
            dma((CHUNKS, n_f - 1)),
            dma((n_f - 1,)),
            dma((n_f - 1,)),
            dma((CHUNKS,)),
            dma((CHUNKS,)),
            dma((CHUNKS, n_z - 1)),
            dma((CHUNKS, n_z - 1)),
            dma((CHUNKS, n_z - 1)),
            dma((CHUNKS, n_z - 1)),
            dma((CHUNKS,)),
            dma((CHUNKS,)),
            dma((4, CHUNKS)),
        ],
        compiler_params=pltpu.CompilerParams(
            collective_id=0, has_side_effects=True, vmem_limit_bytes=51700 * 1024
        ),
        name="mean",
    )(key, act, grads, local, anchor)

    return pl.pallas_call(
        update_kernel,
        out_shape=(
            jax.ShapeDtypeStruct(anchor.shape, anchor.dtype),
            jax.ShapeDtypeStruct(momentum.shape, momentum.dtype),
        ),
        in_specs=[vmem] * 4,
        out_specs=(hbm, hbm),
        scratch_shapes=[
            pltpu.VMEM((2, GROUP * width, depth), jnp.float32),
            pltpu.VMEM((2, GROUP * width, rank), jnp.float32),
            dma((2, 2)),
        ],
        compiler_params=pltpu.CompilerParams(vmem_limit_bytes=32 * 1024 * 1024),
        name="update",
    )(gathered, turned, anchor, momentum)


def in_steps(activations, grad_out, local_weight, anchor, momentum, projection_key):
    inputs = activations[0]
    grads = grad_out[0]
    local = local_weight[0]
    proj = projection(projection_key[0], projection_key[1], grads.shape[1], momentum.shape[1])
    replicas = lax.axis_size("replica")
    scale = float(inputs.shape[0] * lax.axis_size("fsdp")) ** (-0.5)
    drift = anchor - local.astype(jnp.float32)
    columns = lax.all_to_all(inputs, "fsdp", split_axis=1, concat_axis=0, tiled=True)
    projected = jnp.dot(grads.astype(jnp.float32), proj, precision=HIGH)
    grad_part = lax.dot_general(
        columns.astype(jnp.float32),
        lax.all_gather(projected.astype(jnp.bfloat16), "fsdp", axis=0, tiled=True).astype(
            jnp.float32
        ),
        TN,
        precision=HIGH,
        preferred_element_type=jnp.float32,
    )
    local_term = jnp.dot(drift, proj, precision=HIGH) + scale * grad_part
    compressed_mean = lax.psum(local_term, "replica") / replicas
    new_momentum = 0.9 * momentum + compressed_mean
    update = compressed_mean + 0.9 * new_momentum
    new_anchor = anchor - 0.7 * jnp.dot(update, proj.T, precision=HIGH)
    return (new_anchor, new_momentum)


def solution(mesh):
    n_rep, n_f = mesh.shape["replica"], mesh.shape["fsdp"]
    n_y = 2

    def on_device(act, grads, local, anchor, momentum, key):
        rows, depth = anchor.shape
        rank = momentum.shape[1]
        fits = n_rep % n_y == 0 and n_rep > n_y and n_f > 1
        fits = fits and rows % (CHUNKS * n_rep * 16) == 0 and (rows // CHUNKS) % 128 == 0
        fits = fits and act.shape[1] % 16 == 0 and rank % 128 == 0 and depth % rank == 0
        if fits:
            return in_kernels(n_rep, n_y, n_f, act, grads, local, anchor, momentum, key)
        return in_steps(act, grads, local, anchor, momentum, key)

    placed = (
        P("replica", "fsdp", None),
        P("replica", "fsdp", None),
        P("replica", "fsdp", None),
        P("fsdp", None),
        P("fsdp", None),
        P(),
    )
    return jax.shard_map(
        on_device,
        mesh=mesh,
        in_specs=placed,
        out_specs=(P("fsdp", None), P("fsdp", None)),
        check_vma=False,
    )
```

```python
import functools

import jax
import jax.numpy as jnp
from jax import lax
from jax.experimental import pallas as pl
from jax.experimental.pallas import tpu as pltpu
from jax.sharding import PartitionSpec as P

HIGH = lax.Precision.HIGHEST
MESH = pl.DeviceIdType.MESH
CHUNKS = 8
AHEAD = 2
GROUP = 2
DIRECT = 2
PAD = 16
LANES = 128
LEVELS = 32500.0
STEPS = 256.0
TN = (((0,), (0,)), ((), ()))


def projection(word0, word1, rows, cols, first=0, turned=False):
    shape = (cols, rows) if turned else (rows, cols)
    k_index = lax.broadcasted_iota(jnp.int32, shape, int(turned)) + first
    r_index = lax.broadcasted_iota(jnp.int32, shape, int(not turned))
    hashed = word0 + k_index * 668265261 + r_index * 374761393 + word1 * 1103515245
    hashed = jnp.bitwise_xor(hashed, lax.shift_right_logical(hashed, jnp.int32(15)))
    hashed = hashed * 739982445
    hashed = jnp.bitwise_xor(hashed, lax.shift_right_logical(hashed, jnp.int32(12)))
    hashed = hashed * 695938361
    hashed = jnp.bitwise_xor(hashed, lax.shift_right_logical(hashed, jnp.int32(15)))
    level = jnp.bitwise_and(lax.shift_right_logical(hashed, jnp.int32(8)), 65535).astype(
        jnp.float32
    )
    return ((level + 0.5) / 65536.0 - 0.5) * (12.0 / float(cols)) ** 0.5


def split(value):
    high = value.astype(jnp.bfloat16)
    return high, (value - high.astype(jnp.float32)).astype(jnp.bfloat16)


def dot(a, b, dims=(((1,), (0,)), ((), ()))):
    return lax.dot_general(a, b, dims, preferred_element_type=jnp.float32)


def encode(value, refs):
    cols = value.shape[1]
    parts, rows = cols // LANES, value.shape[0] // len(refs)
    top = jnp.max(jnp.abs(value), axis=0, keepdims=True)
    power = jnp.ceil(jnp.log(jnp.maximum(top, 1e-30)) * (STEPS * 1.4426950408889634))
    factor = jnp.exp2(power * (-1.0 / STEPS)) * LEVELS
    coded = jnp.round(value * factor).astype(jnp.int32).astype(jnp.int16)
    line = lax.broadcasted_iota(jnp.int32, (PAD, LANES), 0)
    scales = jnp.zeros((PAD, LANES), jnp.float32)
    for part in range(parts):
        scales = jnp.where(line == part, power[:, part * LANES : (part + 1) * LANES], scales)
    scales = scales.astype(jnp.int32).astype(jnp.int16)
    for n, ref in enumerate(refs):
        for part in range(parts):
            ref[part * rows : (part + 1) * rows, :] = coded[
                n * rows : (n + 1) * rows, part * LANES : (part + 1) * LANES
            ]
        ref[parts * rows :, :] = scales


def decode(ref, cols):
    parts = cols // LANES
    rows = (ref.shape[0] - PAD) // parts
    power = ref[parts * rows :, :].astype(jnp.int32).astype(jnp.float32)
    scale = jnp.exp2(power * (1.0 / STEPS)) * (1.0 / LEVELS)
    return jnp.concatenate(
        [
            ref[part * rows : (part + 1) * rows, :].astype(jnp.int32).astype(jnp.float32)
            * scale[part : part + 1]
            for part in range(parts)
        ],
        axis=1,
    )


def mean_kernel(
    n_rep, n_y, n_f, key_hbm, act, grads, local, anchor, gathered, turned,
    key, proj, columns, weights, own_anchor, base, total, pg, grads_in, y_out, y_in, z_out, z_in,
    act_s, act_r, pg_s, pg_r, y1_s, y1_r, z1_s, z1_r, z2_s, z2_r, y2_s, y2_r, x2_s, x2_r, here,
):
    n_z = n_rep // n_y
    chunks, tokens_all, width = columns.shape
    tokens = tokens_all // n_f
    half = width // n_y
    block = half // n_z
    depth = weights.shape[2]
    rank = pg.shape[1]
    rep = lax.axis_index("replica")
    f = lax.axis_index("fsdp")
    z, y = rep // n_y, rep % n_y
    other = n_y - 1 - y
    y_peer = {"replica": z * n_y + other}
    relayed = chunks - DIRECT

    def z_peer(d):
        return {"replica": ((z + d) % n_z) * n_y + y}

    def cross_peer(d):
        return {"replica": ((z + d) % n_z) * n_y + other}

    barrier = pltpu.get_barrier_semaphore()
    for d in range(1, n_f):
        pl.semaphore_signal(barrier, inc=1, device_id={"fsdp": (f + d) % n_f}, device_id_type=MESH)
    for d in range(1, n_z):
        pl.semaphore_signal(barrier, inc=1, device_id=z_peer(d), device_id_type=MESH)
    for d in range(n_z):
        pl.semaphore_signal(barrier, inc=1, device_id=cross_peer(d), device_id_type=MESH)

    def remote(src, dst, send, recv, device):
        return pltpu.make_async_remote_copy(
            src_ref=src, dst_ref=dst, send_sem=send, recv_sem=recv,
            device_id=device, device_id_type=MESH,
        )

    mine = pl.ds(pl.multiple_of(f * tokens, tokens), tokens)

    def act_copy(c, d):
        g = (f + d) % n_f
        at = pl.ds(pl.multiple_of((g * chunks + c) * width, width), width)
        return remote(
            act.at[0, :, at], columns.at[c, mine, :], act_s.at[c, d - 1], act_r.at[c, d - 1],
            {"fsdp": g},
        )

    def act_own(c):
        at = pl.ds(pl.multiple_of((f * chunks + c) * width, width), width)
        return pltpu.make_async_copy(act.at[0, :, at], columns.at[c, mine, :], here.at[0, c])

    def weight_copy(c):
        at = pl.ds(pl.multiple_of(c * width, width), width)
        return pltpu.make_async_copy(local.at[0, at, :], weights.at[c], here.at[1, c])

    def anchor_copy(c):
        at = pl.ds(pl.multiple_of(c * width + y * half + z * block, block), block)
        return pltpu.make_async_copy(anchor.at[at, :], own_anchor.at[pl.ds(c * block, block), :], here.at[2, c])

    def pg_copy(d):
        return remote(
            pg.at[mine, :], pg.at[mine, :], pg_s.at[d - 1], pg_r.at[d - 1], {"fsdp": (f + d) % n_f}
        )

    def y1_copy(c):
        return remote(y_out.at[c], y_in.at[c], y1_s.at[c], y1_r.at[c], y_peer)

    def z1_copy(c, d):
        return remote(
            z_out.at[c, (z + d) % n_z], z_in.at[c, d - 1], z1_s.at[c, d - 1], z1_r.at[c, d - 1], z_peer(d)
        )

    def z2_copy(c, d):
        return remote(
            gathered.at[c, y, z], gathered.at[c, y, z], z2_s.at[c, d - 1], z2_r.at[c, d - 1],
            z_peer(d),
        )

    def y2_copy(c):
        return remote(gathered.at[c, y], gathered.at[c, y], y2_s.at[c], y2_r.at[c], y_peer)

    def cross_copy(c, d):
        return remote(
            gathered.at[c, y, z], gathered.at[c, y, z], x2_s.at[c, d], x2_r.at[c, d], cross_peer(d)
        )

    fetch = pltpu.make_async_copy(grads.at[0], grads_in, here.at[3, 0])
    fetch.start()
    words = pltpu.make_async_copy(key_hbm, key, here.at[3, 1])
    words.start()
    for c in range(chunks):
        weight_copy(c).start()
        act_own(c).start()
        anchor_copy(c).start()
    pl.semaphore_wait(barrier, n_f + 2 * n_z - 2)
    order = sorted(range(1, n_f), key=lambda d: abs(d - n_f // 2))
    for d in order:
        act_copy(0, d).start()
    words.wait()

    @pl.loop(0, depth, step=rank)
    def _(k):
        at = pl.ds(pl.multiple_of(k, rank), rank)
        high, low = split(projection(key[0], key[1], rank, rank, k))
        proj[at, :rank] = high
        proj[at, rank:] = low

    fetch.wait()
    both = dot(grads_in[...], proj[...])
    pg[mine, :] = (both[:, :rank] + both[:, rank:]).astype(jnp.bfloat16)
    for d in order:
        pg_copy(d).start()
    for c in range(1, min(AHEAD, chunks)):
        for d in order:
            act_copy(c, d).start()

    @pl.loop(0, chunks)
    def _(c):
        weight_copy(c).wait()
        both = dot(weights[c], proj[...])
        total[c] = (both[:, :rank] + both[:, rank:]) * (-1.0 / n_rep)

    for c in range(chunks):
        anchor_copy(c).wait()
    high, low = split(own_anchor[...])
    both = dot(high, proj[...])
    base[...] = both[:, :rank] + both[:, rank:] + dot(low, proj[:, :rank])

    for k in range(0, depth, rank):
        high, low = split(projection(key[0], key[1], rank, rank, k, True))
        turned[:rank, k : k + rank] = high
        turned[rank : 2 * rank, k : k + rank] = low
        turned[2 * rank :, k : k + rank] = high
    for d in range(1, n_f):
        pg_copy(d).wait_recv()
    scale = float(tokens_all) ** (-0.5) / n_rep

    def partial_sum(c):
        act_own(c).wait()
        for d in range(1, n_f):
            act_copy(c, d).wait_recv()

        total[c] += dot(columns[c], pg[...], TN) * scale
        far = pl.ds(pl.multiple_of(other * half, half), half)
        encode(total[c, far, :], [y_out.at[c]])
        y1_copy(c).start()

        @pl.when(c + AHEAD < chunks)
        def _():
            for d in order:
                act_copy(c + AHEAD, d).start()

    def sum_of_pair(c):
        y1_copy(c).wait_recv()
        near = pl.ds(pl.multiple_of(y * half, half), half)
        pair = total[c, near, :] + decode(y_in.at[c], rank)
        total[c, near, :] = pair
        encode(pair, [z_out.at[c, q] for q in range(n_z)])
        for d in range(1, n_z):
            z1_copy(c, d).start()

    def whole_mean(c):
        at = pl.ds(pl.multiple_of(y * half + z * block, block), block)
        own = pl.ds(pl.multiple_of(c * block, block), block)
        value = total[c, at, :] + base[own, :]
        for d in range(1, n_z):
            z1_copy(c, d).wait_recv()
            value += decode(z_in.at[c, d - 1], rank)
        encode(value, [gathered.at[c, y, z]])
        for d in range(1, n_z):
            z2_copy(c, d).start()

        @pl.when(c >= relayed)
        def _():
            for d in range(n_z):
                cross_copy(c, d).start()

    def hand_over(c):
        for d in range(1, n_z):
            z2_copy(c, d).wait_recv()

        @pl.when(c < relayed)
        def _():
            y2_copy(c).start()

    stages = ((partial_sum, 0), (hand_over, 4), (sum_of_pair, 1), (whole_mean, 2))

    @pl.loop(0, chunks + 4)
    def _(t):
        for stage, lag in stages:

            @pl.when(jnp.logical_and(t >= lag, t < chunks + lag))
            def _(stage=stage, lag=lag):
                stage(t - lag)

    for d in range(1, n_f):
        pg_copy(d).wait_send()

    @pl.loop(0, chunks)
    def _(c):
        for d in range(1, n_f):
            act_copy(c, d).wait_send()
        y1_copy(c).wait_send()
        for d in range(1, n_z):
            z1_copy(c, d).wait_send()
            z2_copy(c, d).wait_send()

        @pl.when(c < relayed)
        def _():
            y2_copy(c).wait_send()
            y2_copy(c).wait_recv()

        @pl.when(c >= relayed)
        def _():
            for d in range(n_z):
                cross_copy(c, d).wait_send()
                cross_copy(c, d).wait_recv()


def update_kernel(
    gathered, turned, anchor, momentum, new_anchor, new_momentum, anchor_out, momentum_out, sems
):
    chunks, n_y, n_z = gathered.shape[:3]
    rank = momentum.shape[1]
    steps = chunks // GROUP
    width = momentum.shape[0] // steps

    def stores(c):
        at = pl.ds(pl.multiple_of(c * width, width), width)
        slot = c % 2
        return (
            pltpu.make_async_copy(anchor_out.at[slot], new_anchor.at[at, :], sems.at[0, slot]),
            pltpu.make_async_copy(momentum_out.at[slot], new_momentum.at[at, :], sems.at[1, slot]),
        )

    @pl.loop(0, steps)
    def _(c):
        slot = c % 2

        @pl.when(c >= 2)
        def _():
            for store in stores(c - 2):
                store.wait()

        mean = jnp.concatenate(
            [
                decode(gathered.at[c * GROUP + g, h, q], rank)
                for g in range(GROUP)
                for h in range(n_y)
                for q in range(n_z)
            ],
            axis=0,
        )
        at = pl.ds(pl.multiple_of(c * width, width), width)
        moved = 0.9 * momentum[at, :] + mean
        momentum_out[slot] = moved
        high, low = split(mean + 0.9 * moved)
        step = dot(jnp.concatenate([high, high, low], axis=1), turned[...])
        anchor_out[slot] = anchor[at, :] - 0.7 * step
        for store in stores(c):
            store.start()

    for c in range(max(steps - 2, 0), steps):
        for store in stores(c):
            store.wait()


def in_kernels(n_rep, n_y, n_f, act, grads, local, anchor, momentum, key):
    n_z = n_rep // n_y
    rows, depth = anchor.shape
    rank = momentum.shape[1]
    tokens = act.shape[1]
    width = rows // CHUNKS
    half = width // n_y
    block = half // n_z
    dma = pltpu.SemaphoreType.DMA
    hbm = pl.BlockSpec(memory_space=pltpu.HBM)
    coded = rank // LANES
    vmem = pl.BlockSpec(memory_space=pltpu.VMEM)
    gathered, turned = pl.pallas_call(
        functools.partial(mean_kernel, n_rep, n_y, n_f),
        out_shape=(
            jax.ShapeDtypeStruct((CHUNKS, n_y, n_z, coded * block + PAD, LANES), jnp.int16),
            jax.ShapeDtypeStruct((3 * rank, depth), jnp.bfloat16),
        ),
        in_specs=[hbm] * 5,
        out_specs=(vmem, vmem),
        scratch_shapes=[
            pltpu.SMEM(key.shape, jnp.int32),
            pltpu.VMEM((depth, 2 * rank), jnp.bfloat16),
            pltpu.VMEM((CHUNKS, tokens * n_f, width), jnp.bfloat16),
            pltpu.VMEM((CHUNKS, width, depth), jnp.bfloat16),
            pltpu.VMEM((CHUNKS * block, depth), jnp.float32),
            pltpu.VMEM((CHUNKS * block, rank), jnp.float32),
            pltpu.VMEM((CHUNKS, width, rank), jnp.float32),
            pltpu.VMEM((tokens * n_f, rank), jnp.bfloat16),
            pltpu.VMEM((tokens, depth), jnp.bfloat16),
            pltpu.VMEM((CHUNKS, coded * half + PAD, LANES), jnp.int16),
            pltpu.VMEM((CHUNKS, coded * half + PAD, LANES), jnp.int16),
            pltpu.VMEM((CHUNKS, n_z, coded * block + PAD, LANES), jnp.int16),
            pltpu.VMEM((CHUNKS, n_z - 1, coded * block + PAD, LANES), jnp.int16),
            dma((CHUNKS, n_f - 1)),
            dma((CHUNKS, n_f - 1)),
            dma((n_f - 1,)),
            dma((n_f - 1,)),
            dma((CHUNKS,)),
            dma((CHUNKS,)),
            dma((CHUNKS, n_z - 1)),
            dma((CHUNKS, n_z - 1)),
            dma((CHUNKS, n_z - 1)),
            dma((CHUNKS, n_z - 1)),
            dma((CHUNKS,)),
            dma((CHUNKS,)),
            dma((CHUNKS, n_z)),
            dma((CHUNKS, n_z)),
            dma((4, CHUNKS)),
        ],
        compiler_params=pltpu.CompilerParams(
            collective_id=0, has_side_effects=True, vmem_limit_bytes=51700 * 1024
        ),
        name="mean",
    )(key, act, grads, local, anchor)

    return pl.pallas_call(
        update_kernel,
        out_shape=(
            jax.ShapeDtypeStruct(anchor.shape, anchor.dtype),
            jax.ShapeDtypeStruct(momentum.shape, momentum.dtype),
        ),
        in_specs=[vmem] * 4,
        out_specs=(hbm, hbm),
        scratch_shapes=[
            pltpu.VMEM((2, GROUP * width, depth), jnp.float32),
            pltpu.VMEM((2, GROUP * width, rank), jnp.float32),
            dma((2, 2)),
        ],
        compiler_params=pltpu.CompilerParams(vmem_limit_bytes=32 * 1024 * 1024),
        name="update",
    )(gathered, turned, anchor, momentum)


def in_steps(activations, grad_out, local_weight, anchor, momentum, projection_key):
    inputs = activations[0]
    grads = grad_out[0]
    local = local_weight[0]
    proj = projection(projection_key[0], projection_key[1], grads.shape[1], momentum.shape[1])
    replicas = lax.axis_size("replica")
    scale = float(inputs.shape[0] * lax.axis_size("fsdp")) ** (-0.5)
    drift = anchor - local.astype(jnp.float32)
    columns = lax.all_to_all(inputs, "fsdp", split_axis=1, concat_axis=0, tiled=True)
    projected = jnp.dot(grads.astype(jnp.float32), proj, precision=HIGH)
    grad_part = lax.dot_general(
        columns.astype(jnp.float32),
        lax.all_gather(projected.astype(jnp.bfloat16), "fsdp", axis=0, tiled=True).astype(
            jnp.float32
        ),
        TN,
        precision=HIGH,
        preferred_element_type=jnp.float32,
    )
    local_term = jnp.dot(drift, proj, precision=HIGH) + scale * grad_part
    compressed_mean = lax.psum(local_term, "replica") / replicas
    new_momentum = 0.9 * momentum + compressed_mean
    update = compressed_mean + 0.9 * new_momentum
    new_anchor = anchor - 0.7 * jnp.dot(update, proj.T, precision=HIGH)
    return (new_anchor, new_momentum)


def solution(mesh):
    n_rep, n_f = mesh.shape["replica"], mesh.shape["fsdp"]
    n_y = 2

    def on_device(act, grads, local, anchor, momentum, key):
        rows, depth = anchor.shape
        rank = momentum.shape[1]
        fits = n_rep % n_y == 0 and n_rep > n_y and n_f > 1
        fits = fits and rows % (CHUNKS * n_rep * 16) == 0 and (rows // CHUNKS) % 128 == 0
        fits = fits and act.shape[1] % 16 == 0 and rank % 128 == 0 and depth % rank == 0
        if fits:
            return in_kernels(n_rep, n_y, n_f, act, grads, local, anchor, momentum, key)
        return in_steps(act, grads, local, anchor, momentum, key)

    placed = (
        P("replica", "fsdp", None),
        P("replica", "fsdp", None),
        P("replica", "fsdp", None),
        P("fsdp", None),
        P("fsdp", None),
        P(),
    )
    return jax.shard_map(
        on_device,
        mesh=mesh,
        in_specs=placed,
        out_specs=(P("fsdp", None), P("fsdp", None)),
        check_vma=False,
    )
```

```python
import functools

import jax
import jax.numpy as jnp
from jax import lax
from jax.experimental import pallas as pl
from jax.experimental.pallas import tpu as pltpu
from jax.sharding import PartitionSpec as P

HIGH = lax.Precision.HIGHEST
MESH = pl.DeviceIdType.MESH
CHUNKS = 8
AHEAD = 2
GROUP = 2
PAD = 16
LANES = 128
LEVELS = 32500.0
STEPS = 256.0
TN = (((0,), (0,)), ((), ()))


def projection(word0, word1, rows, cols, first=0, turned=False):
    shape = (cols, rows) if turned else (rows, cols)
    k_index = lax.broadcasted_iota(jnp.int32, shape, int(turned)) + first
    r_index = lax.broadcasted_iota(jnp.int32, shape, int(not turned))
    hashed = word0 + k_index * 668265261 + r_index * 374761393 + word1 * 1103515245
    hashed = jnp.bitwise_xor(hashed, lax.shift_right_logical(hashed, jnp.int32(15)))
    hashed = hashed * 739982445
    hashed = jnp.bitwise_xor(hashed, lax.shift_right_logical(hashed, jnp.int32(12)))
    hashed = hashed * 695938361
    hashed = jnp.bitwise_xor(hashed, lax.shift_right_logical(hashed, jnp.int32(15)))
    level = jnp.bitwise_and(lax.shift_right_logical(hashed, jnp.int32(8)), 65535).astype(
        jnp.float32
    )
    return ((level + 0.5) / 65536.0 - 0.5) * (12.0 / float(cols)) ** 0.5


def split(value):
    high = value.astype(jnp.bfloat16)
    return high, (value - high.astype(jnp.float32)).astype(jnp.bfloat16)


def dot(a, b, dims=(((1,), (0,)), ((), ()))):
    return lax.dot_general(a, b, dims, preferred_element_type=jnp.float32)


def encode(value, refs):
    cols = value.shape[1]
    parts, rows = cols // LANES, value.shape[0] // len(refs)
    top = jnp.max(jnp.abs(value), axis=0, keepdims=True)
    power = jnp.ceil(jnp.log(jnp.maximum(top, 1e-30)) * (STEPS * 1.4426950408889634))
    factor = jnp.exp2(power * (-1.0 / STEPS)) * LEVELS
    coded = jnp.round(value * factor).astype(jnp.int32).astype(jnp.int16)
    line = lax.broadcasted_iota(jnp.int32, (PAD, LANES), 0)
    scales = jnp.zeros((PAD, LANES), jnp.float32)
    for part in range(parts):
        scales = jnp.where(line == part, power[:, part * LANES : (part + 1) * LANES], scales)
    scales = scales.astype(jnp.int32).astype(jnp.int16)
    for n, ref in enumerate(refs):
        for part in range(parts):
            ref[part * rows : (part + 1) * rows, :] = coded[
                n * rows : (n + 1) * rows, part * LANES : (part + 1) * LANES
            ]
        ref[parts * rows :, :] = scales


def decode(ref, cols):
    parts = cols // LANES
    rows = (ref.shape[0] - PAD) // parts
    power = ref[parts * rows :, :].astype(jnp.int32).astype(jnp.float32)
    scale = jnp.exp2(power * (1.0 / STEPS)) * (1.0 / LEVELS)
    return jnp.concatenate(
        [
            ref[part * rows : (part + 1) * rows, :].astype(jnp.int32).astype(jnp.float32)
            * scale[part : part + 1]
            for part in range(parts)
        ],
        axis=1,
    )


def mean_kernel(
    n_rep, n_y, n_f, key_hbm, act, grads, local, anchor, gathered, turned,
    key, proj, columns, weights, own_anchor, base, total, pg, grads_in, y_out, y_in, z_out, z_in,
    act_s, act_r, pg_s, pg_r, y1_s, y1_r, z1_s, z1_r, z2_s, z2_r, y2_s, y2_r, here,
):
    n_z = n_rep // n_y
    chunks, tokens_all, width = columns.shape
    tokens = tokens_all // n_f
    half = width // n_y
    block = half // n_z
    depth = weights.shape[2]
    rank = pg.shape[1]
    rep = lax.axis_index("replica")
    f = lax.axis_index("fsdp")
    z, y = rep // n_y, rep % n_y
    other = n_y - 1 - y
    y_peer = {"replica": z * n_y + other}

    def z_peer(d):
        return {"replica": ((z + d) % n_z) * n_y + y}

    barrier = pltpu.get_barrier_semaphore()
    for d in range(1, n_f):
        pl.semaphore_signal(barrier, inc=1, device_id={"fsdp": (f + d) % n_f}, device_id_type=MESH)
    for d in range(1, n_z):
        pl.semaphore_signal(barrier, inc=1, device_id=z_peer(d), device_id_type=MESH)
    pl.semaphore_signal(barrier, inc=1, device_id=y_peer, device_id_type=MESH)

    def remote(src, dst, send, recv, device):
        return pltpu.make_async_remote_copy(
            src_ref=src, dst_ref=dst, send_sem=send, recv_sem=recv,
            device_id=device, device_id_type=MESH,
        )

    mine = pl.ds(pl.multiple_of(f * tokens, tokens), tokens)

    def act_copy(c, d):
        g = (f + d) % n_f
        at = pl.ds(pl.multiple_of((g * chunks + c) * width, width), width)
        return remote(
            act.at[0, :, at], columns.at[c, mine, :], act_s.at[c, d - 1], act_r.at[c, d - 1],
            {"fsdp": g},
        )

    def act_own(c):
        at = pl.ds(pl.multiple_of((f * chunks + c) * width, width), width)
        return pltpu.make_async_copy(act.at[0, :, at], columns.at[c, mine, :], here.at[0, c])

    def weight_copy(c):
        at = pl.ds(pl.multiple_of(c * width, width), width)
        return pltpu.make_async_copy(local.at[0, at, :], weights.at[c], here.at[1, c])

    def anchor_copy(c):
        at = pl.ds(pl.multiple_of(c * width + y * half + z * block, block), block)
        return pltpu.make_async_copy(anchor.at[at, :], own_anchor.at[pl.ds(c * block, block), :], here.at[2, c])

    def pg_copy(d):
        return remote(
            pg.at[mine, :], pg.at[mine, :], pg_s.at[d - 1], pg_r.at[d - 1], {"fsdp": (f + d) % n_f}
        )

    def y1_copy(c):
        return remote(y_out.at[c], y_in.at[c], y1_s.at[c], y1_r.at[c], y_peer)

    def z1_copy(c, d):
        return remote(
            z_out.at[c, (z + d) % n_z], z_in.at[c, d - 1], z1_s.at[c, d - 1], z1_r.at[c, d - 1], z_peer(d)
        )

    def z2_copy(c, d):
        return remote(
            gathered.at[c, y, z], gathered.at[c, y, z], z2_s.at[c, d - 1], z2_r.at[c, d - 1],
            z_peer(d),
        )

    def y2_copy(c):
        return remote(gathered.at[c, y], gathered.at[c, y], y2_s.at[c], y2_r.at[c], y_peer)

    fetch = pltpu.make_async_copy(grads.at[0], grads_in, here.at[3, 0])
    fetch.start()
    words = pltpu.make_async_copy(key_hbm, key, here.at[3, 1])
    words.start()
    for c in range(chunks):
        weight_copy(c).start()
        act_own(c).start()
        anchor_copy(c).start()
    pl.semaphore_wait(barrier, n_f + n_z - 1)
    order = sorted(range(1, n_f), key=lambda d: abs(d - n_f // 2))
    for d in order:
        act_copy(0, d).start()
    words.wait()

    @pl.loop(0, depth, step=rank)
    def _(k):
        at = pl.ds(pl.multiple_of(k, rank), rank)
        high, low = split(projection(key[0], key[1], rank, rank, k))
        proj[at, :rank] = high
        proj[at, rank:] = low

    fetch.wait()
    both = dot(grads_in[...], proj[...])
    pg[mine, :] = (both[:, :rank] + both[:, rank:]).astype(jnp.bfloat16)
    for d in order:
        pg_copy(d).start()
    for c in range(1, min(AHEAD, chunks)):
        for d in order:
            act_copy(c, d).start()

    @pl.loop(0, chunks)
    def _(c):
        weight_copy(c).wait()
        both = dot(weights[c], proj[...])
        total[c] = (both[:, :rank] + both[:, rank:]) * (-1.0 / n_rep)

    for c in range(chunks):
        anchor_copy(c).wait()
    high, low = split(own_anchor[...])
    both = dot(high, proj[...])
    base[...] = both[:, :rank] + both[:, rank:] + dot(low, proj[:, :rank])

    for k in range(0, depth, rank):
        high, low = split(projection(key[0], key[1], rank, rank, k, True))
        turned[:rank, k : k + rank] = high
        turned[rank : 2 * rank, k : k + rank] = low
        turned[2 * rank :, k : k + rank] = high
    for d in range(1, n_f):
        pg_copy(d).wait_recv()
    scale = float(tokens_all) ** (-0.5) / n_rep

    def partial_sum(c):
        act_own(c).wait()
        for d in range(1, n_f):
            act_copy(c, d).wait_recv()

        total[c] += dot(columns[c], pg[...], TN) * scale
        far = pl.ds(pl.multiple_of(other * half, half), half)
        encode(total[c, far, :], [y_out.at[c]])
        y1_copy(c).start()

        @pl.when(c + AHEAD < chunks)
        def _():
            for d in order:
                act_copy(c + AHEAD, d).start()

    def sum_of_pair(c):
        y1_copy(c).wait_recv()
        near = pl.ds(pl.multiple_of(y * half, half), half)
        pair = total[c, near, :] + decode(y_in.at[c], rank)
        total[c, near, :] = pair
        encode(pair, [z_out.at[c, q] for q in range(n_z)])
        for d in range(1, n_z):
            z1_copy(c, d).start()

    def whole_mean(c):
        at = pl.ds(pl.multiple_of(y * half + z * block, block), block)
        own = pl.ds(pl.multiple_of(c * block, block), block)
        value = total[c, at, :] + base[own, :]
        for d in range(1, n_z):
            z1_copy(c, d).wait_recv()
            value += decode(z_in.at[c, d - 1], rank)
        encode(value, [gathered.at[c, y, z]])
        for d in range(1, n_z):
            z2_copy(c, d).start()

    def hand_over(c):
        for d in range(1, n_z):
            z2_copy(c, d).wait_recv()
        y2_copy(c).start()

    stages = ((partial_sum, 0), (sum_of_pair, 1), (whole_mean, 2), (hand_over, 3))

    @pl.loop(0, chunks + 3)
    def _(t):
        for stage, lag in stages:

            @pl.when(jnp.logical_and(t >= lag, t < chunks + lag))
            def _(stage=stage, lag=lag):
                stage(t - lag)

    for d in range(1, n_f):
        pg_copy(d).wait_send()

    @pl.loop(0, chunks)
    def _(c):
        for d in range(1, n_f):
            act_copy(c, d).wait_send()
        y1_copy(c).wait_send()
        for d in range(1, n_z):
            z1_copy(c, d).wait_send()
            z2_copy(c, d).wait_send()
        y2_copy(c).wait_send()
        y2_copy(c).wait_recv()


def update_kernel(
    gathered, turned, anchor, momentum, new_anchor, new_momentum, anchor_out, momentum_out, sems
):
    chunks, n_y, n_z = gathered.shape[:3]
    rank = momentum.shape[1]
    steps = chunks // GROUP
    width = momentum.shape[0] // steps

    def stores(c):
        at = pl.ds(pl.multiple_of(c * width, width), width)
        slot = c % 2
        return (
            pltpu.make_async_copy(anchor_out.at[slot], new_anchor.at[at, :], sems.at[0, slot]),
            pltpu.make_async_copy(momentum_out.at[slot], new_momentum.at[at, :], sems.at[1, slot]),
        )

    @pl.loop(0, steps)
    def _(c):
        slot = c % 2

        @pl.when(c >= 2)
        def _():
            for store in stores(c - 2):
                store.wait()

        mean = jnp.concatenate(
            [
                decode(gathered.at[c * GROUP + g, h, q], rank)
                for g in range(GROUP)
                for h in range(n_y)
                for q in range(n_z)
            ],
            axis=0,
        )
        at = pl.ds(pl.multiple_of(c * width, width), width)
        moved = 0.9 * momentum[at, :] + mean
        momentum_out[slot] = moved
        high, low = split(mean + 0.9 * moved)
        step = dot(jnp.concatenate([high, high, low], axis=1), turned[...])
        anchor_out[slot] = anchor[at, :] - 0.7 * step
        for store in stores(c):
            store.start()

    for c in range(max(steps - 2, 0), steps):
        for store in stores(c):
            store.wait()


def in_kernels(n_rep, n_y, n_f, act, grads, local, anchor, momentum, key):
    n_z = n_rep // n_y
    rows, depth = anchor.shape
    rank = momentum.shape[1]
    tokens = act.shape[1]
    width = rows // CHUNKS
    half = width // n_y
    block = half // n_z
    dma = pltpu.SemaphoreType.DMA
    hbm = pl.BlockSpec(memory_space=pltpu.HBM)
    coded = rank // LANES
    vmem = pl.BlockSpec(memory_space=pltpu.VMEM)
    gathered, turned = pl.pallas_call(
        functools.partial(mean_kernel, n_rep, n_y, n_f),
        out_shape=(
            jax.ShapeDtypeStruct((CHUNKS, n_y, n_z, coded * block + PAD, LANES), jnp.int16),
            jax.ShapeDtypeStruct((3 * rank, depth), jnp.bfloat16),
        ),
        in_specs=[hbm] * 5,
        out_specs=(vmem, vmem),
        scratch_shapes=[
            pltpu.SMEM(key.shape, jnp.int32),
            pltpu.VMEM((depth, 2 * rank), jnp.bfloat16),
            pltpu.VMEM((CHUNKS, tokens * n_f, width), jnp.bfloat16),
            pltpu.VMEM((CHUNKS, width, depth), jnp.bfloat16),
            pltpu.VMEM((CHUNKS * block, depth), jnp.float32),
            pltpu.VMEM((CHUNKS * block, rank), jnp.float32),
            pltpu.VMEM((CHUNKS, width, rank), jnp.float32),
            pltpu.VMEM((tokens * n_f, rank), jnp.bfloat16),
            pltpu.VMEM((tokens, depth), jnp.bfloat16),
            pltpu.VMEM((CHUNKS, coded * half + PAD, LANES), jnp.int16),
            pltpu.VMEM((CHUNKS, coded * half + PAD, LANES), jnp.int16),
            pltpu.VMEM((CHUNKS, n_z, coded * block + PAD, LANES), jnp.int16),
            pltpu.VMEM((CHUNKS, n_z - 1, coded * block + PAD, LANES), jnp.int16),
            dma((CHUNKS, n_f - 1)),
            dma((CHUNKS, n_f - 1)),
            dma((n_f - 1,)),
            dma((n_f - 1,)),
            dma((CHUNKS,)),
            dma((CHUNKS,)),
            dma((CHUNKS, n_z - 1)),
            dma((CHUNKS, n_z - 1)),
            dma((CHUNKS, n_z - 1)),
            dma((CHUNKS, n_z - 1)),
            dma((CHUNKS,)),
            dma((CHUNKS,)),
            dma((4, CHUNKS)),
        ],
        compiler_params=pltpu.CompilerParams(
            collective_id=0, has_side_effects=True, vmem_limit_bytes=51700 * 1024
        ),
        name="mean",
    )(key, act, grads, local, anchor)

    return pl.pallas_call(
        update_kernel,
        out_shape=(
            jax.ShapeDtypeStruct(anchor.shape, anchor.dtype),
            jax.ShapeDtypeStruct(momentum.shape, momentum.dtype),
        ),
        in_specs=[vmem] * 4,
        out_specs=(hbm, hbm),
        scratch_shapes=[
            pltpu.VMEM((2, GROUP * width, depth), jnp.float32),
            pltpu.VMEM((2, GROUP * width, rank), jnp.float32),
            dma((2, 2)),
        ],
        compiler_params=pltpu.CompilerParams(vmem_limit_bytes=32 * 1024 * 1024),
        name="update",
    )(gathered, turned, anchor, momentum)


def in_steps(activations, grad_out, local_weight, anchor, momentum, projection_key):
    inputs = activations[0]
    grads = grad_out[0]
    local = local_weight[0]
    proj = projection(projection_key[0], projection_key[1], grads.shape[1], momentum.shape[1])
    replicas = lax.axis_size("replica")
    scale = float(inputs.shape[0] * lax.axis_size("fsdp")) ** (-0.5)
    drift = anchor - local.astype(jnp.float32)
    columns = lax.all_to_all(inputs, "fsdp", split_axis=1, concat_axis=0, tiled=True)
    projected = jnp.dot(grads.astype(jnp.float32), proj, precision=HIGH)
    grad_part = lax.dot_general(
        columns.astype(jnp.float32),
        lax.all_gather(projected.astype(jnp.bfloat16), "fsdp", axis=0, tiled=True).astype(
            jnp.float32
        ),
        TN,
        precision=HIGH,
        preferred_element_type=jnp.float32,
    )
    local_term = jnp.dot(drift, proj, precision=HIGH) + scale * grad_part
    compressed_mean = lax.psum(local_term, "replica") / replicas
    new_momentum = 0.9 * momentum + compressed_mean
    update = compressed_mean + 0.9 * new_momentum
    new_anchor = anchor - 0.7 * jnp.dot(update, proj.T, precision=HIGH)
    return (new_anchor, new_momentum)


def solution(mesh):
    n_rep, n_f = mesh.shape["replica"], mesh.shape["fsdp"]
    n_y = 2

    def on_device(act, grads, local, anchor, momentum, key):
        rows, depth = anchor.shape
        rank = momentum.shape[1]
        fits = n_rep % n_y == 0 and n_rep > n_y and n_f > 1
        fits = fits and rows % (CHUNKS * n_rep * 16) == 0 and (rows // CHUNKS) % 128 == 0
        fits = fits and act.shape[1] % 16 == 0 and rank % 128 == 0 and depth % rank == 0
        if fits:
            return in_kernels(n_rep, n_y, n_f, act, grads, local, anchor, momentum, key)
        return in_steps(act, grads, local, anchor, momentum, key)

    placed = (
        P("replica", "fsdp", None),
        P("replica", "fsdp", None),
        P("replica", "fsdp", None),
        P("fsdp", None),
        P("fsdp", None),
        P(),
    )
    return jax.shard_map(
        on_device,
        mesh=mesh,
        in_specs=placed,
        out_specs=(P("fsdp", None), P("fsdp", None)),
        check_vma=False,
    )
```
